32 devices in a mesh: dp: 8 (over z, y), tensor: 4 (over x, core).
Axes of the slice: x: 2, y: 2, z: 4, core: 2. Of those that a mesh axis runs over, the one named last changes fastest.
Arguments:
- global_tokens: bfloat16 [2, 32, 196, 384], P(None, ('dp', 'tensor')), may hold values from -6 to 6
- local_tokens: bfloat16 [2, 128, 36, 384], P(None, ('dp', 'tensor')), may hold values from -6 to 6
- global_cotangent: bfloat16 [2, 32, 196, 384], P(None, ('dp', 'tensor')), may hold values from -6 to 6
- local_cotangent: bfloat16 [2, 128, 36, 384], P(None, ('dp', 'tensor')), may hold values from -6 to 6
- up_weight: float32 [2, 384, 1536], P(None, 'dp', 'tensor'), may hold values from -0.3125 to 0.3125
- down_weight: float32 [2, 1536, 384], P(None, 'tensor', 'dp'), may hold values from -0.15625 to 0.15625
- filters: float32 [2, 2, 14, 8, 384], replicated, may hold values from -6 to 6
- resize: float32 [24, 112], replicated, may hold values from -0.5 to 0.5
- vectors: float32 [2, 5, 384], replicated, as said below
- hidden_bias: float32 [2, 1536], replicated, may hold values from -2 to 2
- up_momentum: float32 [2, 384, 1536], P(None, 'dp', 'tensor'), as said below
- down_momentum: float32 [2, 1536, 384], P(None, 'tensor', 'dp'), as said below
- filter_means: float32 [2, 2, 14, 8, 384], replicated, as said below
- filter_squares: float32 [2, 2, 14, 8, 384], replicated, as said below
- vector_means: float32 [2, 5, 384], replicated, as said below
- vector_squares: float32 [2, 5, 384], replicated, as said below
- bias_means: float32 [2, 1536], replicated, as said below
- bias_squares: float32 [2, 1536], replicated, as said below
Outputs:
- global_output: bfloat16 [2, 32, 196, 384], P(None, ('dp', 'tensor'))
- local_output: bfloat16 [2, 128, 36, 384], P(None, ('dp', 'tensor'))
- global_gradient: float32 [2, 32, 196, 384], P(None, ('dp', 'tensor'))
- local_gradient: float32 [2, 128, 36, 384], P(None, ('dp', 'tensor'))
- up_velocity: float32 [2, 384, 1536], P(None, 'dp', 'tensor')
- up_master: float32 [2, 384, 1536], P(None, 'dp', 'tensor')
- down_velocity: float32 [2, 1536, 384], P(None, 'tensor', 'dp')
- down_master: float32 [2, 1536, 384], P(None, 'tensor', 'dp')
- filter_mean: float32 [2, 2, 14, 8, 384], replicated
- filter_square: float32 [2, 2, 14, 8, 384], replicated
- filter_master: float32 [2, 2, 14, 8, 384], replicated
- vector_mean: float32 [2, 5, 384], replicated
- vector_square: float32 [2, 5, 384], replicated
- vector_master: float32 [2, 5, 384], replicated
- bias_mean: float32 [2, 1536], replicated
- bias_square: float32 [2, 1536], replicated
- bias_master: float32 [2, 1536], replicated
The draws below stay inside these ranges and needn't reach their ends.
Inputs may be any that keep to these rules, and one draw needn't show every extreme that they name: `vectors`: rows 0 and 2 of each block are gains between 0.7 and 1.3, rows 1, 3 and 4 shifts and biases. `up_momentum`: of the size of the summed gradient, both signs. `down_momentum`: of the size of the summed gradient, both signs. `filter_means`: both signs. `filter_squares`: positive. `vector_means`: both signs. `vector_squares`: positive. `bias_means`: both signs. `bias_squares`: positive.
All inputs are finite; a program needn't handle non-finite values.
Results may differ from the reference program's by a relative error of at most 0.011.
Values may be sent and summed in bfloat16 or wider, within the bound.
No kernel may reach another device: no remote copies, remote signals or barrier semaphores. Data moves between devices by JAX's collectives and lax.ppermute only.
A program may use at most 128 MiB of HBM per device.

```python
import math
import jax
import jax.numpy as jnp
from jax import lax

D = 384
FF = 1536
GRID = 14
FREQ = 8
LGRID = 6
LFREQ = 4
TOKG = 196
TOKL = 36
GSPEC = 112
LSPEC = 24
MICRO = 2
LAYERS = 2
NS_STEPS = 2
STEP = 5
NG = 32
NL = 128
TOKENS_ALL = 21760


def first_moment(key, shape, size):
    return size / 9.0 * jax.random.normal(key, shape, jnp.float32)


def second_moment(key, shape, size):
    expo = jax.random.uniform(key, shape, jnp.float32, math.log(0.5), math.log(8.0))
    return 0.05 / 0.95 * size * size * jnp.exp(expo)


def draw_vectors(key, part):
    key = jax.random.fold_in(key, 11)
    gain_key, shift_key = jax.random.split(key)
    gains = 1.0 + 0.3 * jax.random.uniform(gain_key, (LAYERS, 5, D), jnp.float32, -1.0, 1.0)
    shifts = 0.3 * jax.random.normal(shift_key, (LAYERS, 5, D), jnp.float32)
    row_index = jnp.arange(5)[None, :, None]
    return jnp.where((row_index == 0) | (row_index == 2), gains, shifts)


def draw_up_momentum(key, part):
    key = jax.random.fold_in(key, 12)
    return 0.2 * math.sqrt(TOKENS_ALL) * jax.random.normal(key, (LAYERS, D, FF), jnp.float32)


def draw_down_momentum(key, part):
    key = jax.random.fold_in(key, 13)
    return 0.6 * math.sqrt(TOKENS_ALL) * jax.random.normal(key, (LAYERS, FF, D), jnp.float32)


def draw_filter_means(key, part):
    key = jax.random.fold_in(key, 14)
    return first_moment(key, (LAYERS, 2, GRID, FREQ, D), 0.05 * math.sqrt(TOKENS_ALL))


def draw_filter_squares(key, part):
    key = jax.random.fold_in(key, 15)
    return second_moment(key, (LAYERS, 2, GRID, FREQ, D), 0.05 * math.sqrt(TOKENS_ALL))


def draw_vector_means(key, part):
    key = jax.random.fold_in(key, 16)
    return first_moment(key, (LAYERS, 5, D), 0.5 * math.sqrt(TOKENS_ALL))


def draw_vector_squares(key, part):
    key = jax.random.fold_in(key, 17)
    return second_moment(key, (LAYERS, 5, D), 0.5 * math.sqrt(TOKENS_ALL))


def draw_bias_means(key, part):
    key = jax.random.fold_in(key, 18)
    return first_moment(key, (LAYERS, FF), 0.2 * math.sqrt(TOKENS_ALL))


def draw_bias_squares(key, part):
    key = jax.random.fold_in(key, 19)
    return second_moment(key, (LAYERS, FF), 0.2 * math.sqrt(TOKENS_ALL))


def level_of(own_key, extent, cuts, smallest, high):
    level, own = 1.0, jax.random.fold_in(own_key, 6)
    for dim, parts in cuts:
        draws = jnp.exp(jax.random.uniform(jax.random.fold_in(own, dim), (parts,), jnp.float32, smallest / len(cuts), high / len(cuts)))
        level = level * jnp.repeat(draws, extent[dim] // parts).reshape([-1 if axis == dim else 1 for axis in range(len(extent))])
    return level


def normal_values(own_key, dims, deviation, limit, cuts=(), kind=jnp.bfloat16):
    loudness = level_of(own_key, dims, cuts, -0.22, 0.18) if cuts else 1.0
    values = jax.random.normal(own_key, dims, jnp.float32) * deviation * loudness
    return jnp.minimum(jnp.maximum(values, -limit), limit).astype(kind)


def setup_inputs(seed: int = 0) -> dict:
    seeds = jax.random.split(jax.random.key(seed), 19)
    global_tokens = normal_values(seeds[0], (MICRO, NG, TOKG, D), 1.0, 6.0, ((1, 32),))
    local_tokens = normal_values(seeds[1], (MICRO, NL, TOKL, D), 1.0, 6.0, ((1, 32),))
    global_cotangent = normal_values(seeds[2], (MICRO, NG, TOKG, D), 1.0, 6.0, ((1, 32),))
    local_cotangent = normal_values(seeds[3], (MICRO, NL, TOKL, D), 1.0, 6.0, ((1, 32),))
    up_weight = normal_values(seeds[4], (LAYERS, D, FF), D ** -0.5, 0.3125, ((1, 8), (2, 4)), jnp.float32)
    down_weight = normal_values(seeds[5], (LAYERS, FF, D), FF ** -0.5, 0.15625, ((1, 4), (2, 8)), jnp.float32)
    filters = normal_values(seeds[6], (LAYERS, 2, GRID, FREQ, D), 1.0, 6.0, (), jnp.float32)
    resize = normal_values(seeds[7], (LSPEC, GSPEC), GSPEC ** -0.5, 0.5, (), jnp.float32)
    vectors = draw_vectors(jax.random.fold_in(seeds[18], 71), 0)
    hidden_bias = normal_values(seeds[9], (LAYERS, FF), 0.3, 2.0, (), jnp.float32)
    up_momentum = draw_up_momentum(jax.random.fold_in(seeds[18], 71), 0)
    down_momentum = draw_down_momentum(jax.random.fold_in(seeds[18], 71), 0)
    filter_means = draw_filter_means(jax.random.fold_in(seeds[18], 71), 0)
    filter_squares = draw_filter_squares(jax.random.fold_in(seeds[18], 71), 0)
    vector_means = draw_vector_means(jax.random.fold_in(seeds[18], 71), 0)
    vector_squares = draw_vector_squares(jax.random.fold_in(seeds[18], 71), 0)
    bias_means = draw_bias_means(jax.random.fold_in(seeds[18], 71), 0)
    bias_squares = draw_bias_squares(jax.random.fold_in(seeds[18], 71), 0)
    return dict(global_tokens=global_tokens, local_tokens=local_tokens, global_cotangent=global_cotangent, local_cotangent=local_cotangent, up_weight=up_weight, down_weight=down_weight, filters=filters, resize=resize, vectors=vectors, hidden_bias=hidden_bias, up_momentum=up_momentum, down_momentum=down_momentum, filter_means=filter_means, filter_squares=filter_squares, vector_means=vector_means, vector_squares=vector_squares, bias_means=bias_means, bias_squares=bias_squares)


@jax.custom_vjp
def low(v):
    return lax.optimization_barrier(v.astype(jnp.bfloat16)).astype(jnp.float32)

@jax.custom_vjp
def low_back(v):
    return v

def low_keep(v):
    return (low(v), None)

def low_pass(kept, grad):
    return (grad,)

def back_keep(v):
    return (v, None)

def back_low(kept, grad):
    return (low(grad),)
low.defvjp(low_keep, low_pass)
low_back.defvjp(back_keep, back_low)
highest = lax.Precision.HIGHEST
epsilon_norm = 1e-06
ns_a = 3.4445
ns_b = -4.775
ns_c = 2.0315
momentum_decay = 0.95
muon_rate = 0.25
muon_decay = 0.01
adam_one = 0.9
adam_two = 0.95
adam_rate = 0.25
adam_decay = 0.01
adam_floor = 1e-08

def layer_norm(values, gain, shift):
    center = values - lax.optimization_barrier(jnp.mean(values, -1, keepdims=True))
    spread = lax.optimization_barrier(jnp.mean(center * center, -1, keepdims=True))
    return center * lax.rsqrt(spread + epsilon_norm) * gain + shift

def grid_filter(field, real_part, imag_part, grid):
    count = field.shape[0]
    square = field.reshape(count, grid, grid, field.shape[-1])
    spectrum = jnp.fft.rfft2(square, axes=(1, 2))
    result = jnp.fft.irfft2(spectrum * (real_part + 1j * imag_part), s=(grid, grid), axes=(1, 2))
    return result.real.reshape(field.shape).astype(field.dtype)

def orthogonalize(matrix):
    x = matrix / (jnp.sqrt(jnp.sum(matrix * matrix)) + 1e-07)
    for step_index in range(NS_STEPS):
        gram = jnp.dot(x, x.T, precision=highest, preferred_element_type=jnp.float32)
        poly = ns_b * gram + ns_c * jnp.dot(gram, gram, precision=highest, preferred_element_type=jnp.float32)
        x = ns_a * x + jnp.dot(poly, x, precision=highest, preferred_element_type=jnp.float32)
    return x

def adam_update(weight, grad, first, second):
    first_new = adam_one * first + (1.0 - adam_one) * grad
    second_new = adam_two * second + (1.0 - adam_two) * grad * grad
    first_hat = first_new / (1.0 - adam_one ** STEP)
    second_hat = second_new / (1.0 - adam_two ** STEP)
    weight_new = weight * (1.0 - adam_rate * adam_decay) - adam_rate * first_hat / (jnp.sqrt(second_hat) + adam_floor)
    return (first_new, second_new, weight_new)

def reference(global_tokens, local_tokens, global_cotangent, local_cotangent, up_weight, down_weight, filters, resize, vectors, hidden_bias, up_momentum, down_momentum, filter_means, filter_squares, vector_means, vector_squares, bias_means, bias_squares):

    def forward(params, global_rows, local_rows):
        up_all, down_all, filter_all, vector_all, bias_all = params
        for layer in range(LAYERS):
            up_low = low(up_all[layer])
            down_low = low(down_all[layer])
            vec = vector_all[layer]
            local_real = jnp.dot(resize, filter_all[layer, 0].reshape(GSPEC, D), precision=highest, preferred_element_type=jnp.float32).reshape(LGRID, LFREQ, D)
            local_imag = jnp.dot(resize, filter_all[layer, 1].reshape(GSPEC, D), precision=highest, preferred_element_type=jnp.float32).reshape(LGRID, LFREQ, D)

            def branch(rows, grid, real_part, imag_part):
                normed = layer_norm(rows, vec[0], vec[1])
                filtered = grid_filter(normed, real_part, imag_part, grid)
                mixed = low(layer_norm(filtered, vec[2], vec[3]))
                flat = mixed.reshape(-1, D)
                preact = low_back(jnp.dot(flat, up_low, precision=highest, preferred_element_type=jnp.float32) + bias_all[layer])
                activated = low(jax.nn.gelu(preact, approximate=False))
                result = low_back(jnp.dot(activated, down_low, precision=highest, preferred_element_type=jnp.float32) + vec[4])
                return rows + result.reshape(rows.shape)
            global_rows = branch(global_rows, GRID, filter_all[layer, 0], filter_all[layer, 1])
            local_rows = branch(local_rows, LGRID, local_real, local_imag)
        return (global_rows, local_rows)
    params = (up_weight, down_weight, filters, vectors, hidden_bias)
    totals = jax.tree.map(jnp.zeros_like, params)
    global_outs, local_outs, global_grads, local_grads = ([], [], [], [])
    for micro_step in range(MICRO):
        outputs, pull = jax.vjp(forward, params, global_tokens[micro_step].astype(jnp.float32), local_tokens[micro_step].astype(jnp.float32))
        grads, global_back, local_back = pull((global_cotangent[micro_step].astype(jnp.float32), local_cotangent[micro_step].astype(jnp.float32)))
        totals = jax.tree.map(lambda a, b: a + b, totals, grads)
        global_outs.append(outputs[0].astype(jnp.bfloat16))
        local_outs.append(outputs[1].astype(jnp.bfloat16))
        global_grads.append(global_back)
        local_grads.append(local_back)
    grad_up, grad_down, grad_filters, grad_vectors, grad_bias = totals
    up_velocity = momentum_decay * up_momentum + grad_up
    down_velocity = momentum_decay * down_momentum + grad_down
    muon_scale = 0.2 * math.sqrt(max(D, FF))
    up_orth = jnp.stack([orthogonalize(up_velocity[layer]) for layer in range(LAYERS)])
    down_orth = jnp.stack([orthogonalize(down_velocity[layer].T).T for layer in range(LAYERS)])
    up_master = up_weight * (1.0 - muon_rate * muon_decay) - muon_rate * muon_scale * up_orth
    down_master = down_weight * (1.0 - muon_rate * muon_decay) - muon_rate * muon_scale * down_orth
    filter_mean, filter_square, filter_master = adam_update(filters, grad_filters, filter_means, filter_squares)
    vector_mean, vector_square, vector_master = adam_update(vectors, grad_vectors, vector_means, vector_squares)
    bias_mean, bias_square, bias_master = adam_update(hidden_bias, grad_bias, bias_means, bias_squares)
    return (jnp.stack(global_outs), jnp.stack(local_outs), jnp.stack(global_grads), jnp.stack(local_grads), up_velocity, up_master, down_velocity, down_master, filter_mean, filter_square, filter_master, vector_mean, vector_square, vector_master, bias_mean, bias_square, bias_master)
```

```python
import math

import jax
import jax.numpy as jnp
import numpy as np
from jax import lax
from jax.experimental import pallas as pl
from jax.experimental.pallas import tpu as pltpu
from jax.sharding import PartitionSpec as P

D = 384
FF = 1536
GRID = 14
LGRID = 6
TOKG = GRID * GRID
TOKL = LGRID * LGRID
GSPEC = 112
LSPEC = 24
STEP = 5
TILE = 256
SCALE = 1.15e9
MIB = 1024 * 1024

high = lax.Precision.HIGH
epsilon_norm = 1e-06
ns_a = 3.4445
ns_b = -4.775
ns_c = 2.0315
momentum_decay = 0.95
muon_rate = 0.25
muon_decay = 0.01
adam_one = 0.9
adam_two = 0.95
adam_rate = 0.25
adam_decay = 0.01
adam_floor = 1e-08
contract_last = (((1,), (1,)), ((), ()))
f32 = jnp.float32
bf16 = jnp.bfloat16


def round_up(value, unit):
    return (value + unit - 1) // unit * unit


def dft_table(grid, copies, rows):
    freq_count = grid // 2 + 1
    spec = np.arange(grid * freq_count)
    cell = np.arange(grid * grid)
    phase = (
        np.outer(spec // freq_count, cell // grid) + np.outer(spec % freq_count, cell % grid)
    ) % grid
    theta = 2.0 * np.pi / grid * phase
    eye = np.eye(copies)
    table = np.concatenate([np.kron(eye, np.cos(theta)), np.kron(eye, -np.sin(theta))], 0)
    return np.pad(table, ((0, 0), (0, rows - table.shape[1]))).astype(np.float32)


def spectral_weight(grid, rows):
    freq_count = grid // 2 + 1
    second = lax.rem(lax.broadcasted_iota(jnp.int32, (rows, D), 0), jnp.int32(freq_count))
    once = (second == 0) | (2 * second == grid)
    return jnp.where(once, 1.0, 2.0).astype(f32) / (grid * grid)


class Plan:
    def __init__(self, micro, global_images, local_images):
        self.micro = micro
        self.group = 4 if local_images % 4 == 0 else local_images
        self.g_rows = round_up(TOKG, 16)
        self.l_rows = round_up(self.group * TOKL, 16)
        self.segments = []
        row = spec = 0
        for m in range(micro):
            for image in range(global_images):
                self.segments.append(("g", m, image, row, self.g_rows, spec, GSPEC))
                row += self.g_rows
                spec += 2 * GSPEC
            for image in range(0, local_images, self.group):
                half = self.group * LSPEC
                self.segments.append(("l", m, image, row, self.l_rows, spec, half))
                row += self.l_rows
                spec += 2 * half
        self.rows = row
        self.spec = spec
        self.tables = {
            "g": dft_table(GRID, 1, self.g_rows), "l": dft_table(LGRID, self.group, self.l_rows)
        }
        self.grids = {"g": GRID, "l": LGRID}


def dot(a, b, precision=None):
    return jnp.dot(a, b, preferred_element_type=f32, precision=precision)


def dot_last(a, b):
    return lax.dot_general(a, b, contract_last, preferred_element_type=f32)


def load_rows(plan, seg, dst, g_ref, l_ref):
    kind, m, image, row, rows, _, _ = seg
    if kind == "g":
        if rows != TOKG:
            start = TOKG // 8 * 8
            dst[row + start : row + rows] = jnp.zeros((rows - start, D), f32)
        dst[row : row + TOKG] = g_ref[m, image].astype(f32)
    else:
        used = plan.group * TOKL
        if rows != used:
            start = used // 8 * 8
            dst[row + start : row + rows] = jnp.zeros((rows - start, D), f32)
        for i in range(plan.group):
            dst[row + i * TOKL : row + (i + 1) * TOKL] = l_ref[m, image + i].astype(f32)


def store_rows(plan, seg, src, g_ref, l_ref, micro_inner):
    kind, m, image, row, _, _, _ = seg
    if kind == "g":
        value = src[row : row + TOKG].astype(g_ref.dtype)
        if micro_inner:
            g_ref[image, :, m, :] = value
        else:
            g_ref[m, :, image, :] = value
    else:
        for i in range(plan.group):
            value = src[row + i * TOKL : row + (i + 1) * TOKL].astype(l_ref.dtype)
            l_ref[m, :, image + i, :] = value


def normalize(v):
    center = v - jnp.mean(v, -1, keepdims=True)
    scale = lax.rsqrt(jnp.mean(center * center, -1, keepdims=True) + epsilon_norm)
    return center * scale, scale


def normalize_back(dout, gain, normal, scale):
    dn = dout * gain
    return scale * (
        dn
        - jnp.mean(dn, -1, keepdims=True)
        - normal * jnp.mean(dn * normal, -1, keepdims=True)
    )


@jax.tree_util.register_pytree_node_class
class Box(dict):
    __getattr__ = dict.__getitem__
    __setattr__ = dict.__setitem__

    def tree_flatten(self):
        keys = tuple(sorted(self))
        return [self[k] for k in keys], keys

    @classmethod
    def tree_unflatten(cls, keys, values):
        return cls(zip(keys, values))


def struct(shape, dtype):
    return jax.ShapeDtypeStruct(shape, dtype)


class Far:
    def __init__(self, array):
        self.array = array


def far(tree):
    return jax.tree.map(Far, tree)


def call(body, ins, outs, scratch=None, sems=None, weight=0, limit=32 * MIB, aliases=None):
    scratch = {} if scratch is None else scratch
    sems = {} if sems is None else sems
    in_leaves, in_tree = jax.tree.flatten(ins)
    out_leaves, out_tree = jax.tree.flatten(outs)
    scratch_leaves, scratch_tree = jax.tree.flatten(scratch)
    sem_leaves, sem_tree = jax.tree.flatten(sems)

    def kernel(*refs):
        cuts = np.cumsum([len(in_leaves), len(out_leaves), len(scratch_leaves)])
        parts = [refs[: cuts[0]], refs[cuts[0] : cuts[1]], refs[cuts[1] : cuts[2]], refs[cuts[2] :]]
        trees = [in_tree, out_tree, scratch_tree, sem_tree]
        body(*(jax.tree.unflatten(t, p) for t, p in zip(trees, parts)))

    def spec(leaf):
        if isinstance(leaf, Far):
            return pl.BlockSpec(memory_space=pl.ANY)
        return pl.BlockSpec(memory_space=pltpu.SMEM if leaf.dtype == jnp.int32 else pltpu.VMEM)

    def plain(leaf):
        return leaf.array if isinstance(leaf, Far) else leaf

    total = sum(
        math.prod(plain(a).shape) * plain(a).dtype.itemsize for a in in_leaves + out_leaves
    )
    result = pl.pallas_call(
        kernel,
        out_shape=[plain(a) for a in out_leaves],
        in_specs=[spec(a) for a in in_leaves],
        out_specs=[spec(a) for a in out_leaves],
        scratch_shapes=[pltpu.VMEM(a.shape, a.dtype) for a in scratch_leaves]
        + [pltpu.SemaphoreType.DMA((n,)) for n in sem_leaves],
        input_output_aliases={} if aliases is None else aliases,
        compiler_params=pltpu.CompilerParams(vmem_limit_bytes=limit),
        cost_estimate=pl.CostEstimate(
            flops=int(weight * SCALE), bytes_accessed=total if weight else 0, transcendentals=0
        ),
    )(*(plain(a) for a in in_leaves))
    return jax.tree.unflatten(out_tree, result)


def gate(arrays, token):
    count = len(arrays)
    return pl.pallas_call(
        lambda *refs: None,
        out_shape=[struct(a.shape, a.dtype) for a in arrays],
        in_specs=[pl.BlockSpec(memory_space=pl.ANY)] * (count + 1),
        out_specs=[pl.BlockSpec(memory_space=pl.ANY)] * count,
        input_output_aliases={i: i for i in range(count)},
        compiler_params=pltpu.CompilerParams(vmem_limit_bytes=MIB),
    )(*arrays, token)


def start_copy(src, dst, sem):
    pltpu.make_async_copy(src, dst, sem).start()


def wait_copy(like, sem):
    pltpu.make_async_copy(like, like, sem).wait()


def join(arrays, token=()):
    each, rows, _ = arrays[0].shape

    def body(ins, outs, s, sems):
        for i, array in enumerate(ins.arrays):
            for j in range(each):
                outs[i * each + j] = array[j]

    shape = struct((each * len(arrays), rows, D), bf16)
    return call(body, Box(arrays=arrays, token=far(token)), shape, limit=8 * MIB)


class Net:
    def __init__(self, parts, across):
        self.parts, self.across = parts, across
        self.devices = parts * across
        self.bits = self.devices.bit_length() - 1
        self.power = 2**self.bits == self.devices
        self.stages = [(1, 2)]
        bit = 1
        while bit < self.bits:
            width = min(2, self.bits - bit)
            self.stages.append((2**bit, 2**width))
            bit += width

    def me(self):
        return lax.axis_index("dp") * self.across + lax.axis_index("tensor")

    def swap(self, array, mask):
        pairs = [(i, i ^ mask) for i in range(self.devices)]
        return lax.ppermute(array, ("dp", "tensor"), pairs)

    def masks(self, first):
        found = [0]
        for unit, size in reversed(self.stages[first:]):
            found = [i * unit + m for i in range(size) for m in found]
        return found

    def place(self, me, mask):
        other = me ^ mask
        return other >> (self.across.bit_length() - 1), other & (self.across - 1)

    def stack(self, array, index, token=()):
        unit, size = self.stages[index]
        return join([array] + [self.swap(array, i * unit) for i in range(1, size)], token)

    def gather_far(self, chunk, token=()):
        for index in reversed(range(2, len(self.stages))):
            chunk = self.stack(chunk, index, token)
        return chunk

    def gather_bits(self, chunk, tokens=((), ())):
        masks = [0]
        first = self.stages[1][0] * self.stages[1][1]
        bits = [b for b in range(self.bits) if 2**b >= first]
        for bit in reversed(bits):
            token = tokens[1] if bit == bits[0] else tokens[0] if bit == bits[-1] else ()
            chunk = join([chunk, self.swap(chunk, 2**bit)], token)
            masks = masks + [2**bit + m for m in masks]
        return chunk, masks

    def gather_plane(self, current):
        unit, size = self.stages[1]
        return [current] + [self.swap(current, i * unit) for i in range(1, size)]

    def gather_core(self, pieces):
        return pieces + [self.swap(array, 1) for array in pieces]

    def exchange(self, index, arrays):
        unit, size = self.stages[index]
        return [arrays[0]] + [self.swap(arrays[i], i * unit) for i in range(1, size)]


def add_terms(terms, at):
    total = terms[0][at].astype(f32)
    for term in terms[1:]:
        total = total + term[at].astype(f32)
    return total


def pair(total):
    first = total.astype(bf16).astype(f32)
    return jnp.concatenate([first, total - first], 0).astype(bf16)


def add_pairs(terms, at):
    total = add_terms(terms, at)
    half = total.shape[0] // 2
    return total[:half] + total[half:]


def sum_stage(terms, pairs, cuts, pairs_in=0, token=(), weight=0):
    count, rows, _ = terms[0].shape
    rows -= pairs_in
    each = count // cuts
    extra = pairs[0].shape[1] if pairs else pairs_in

    def body(ins, outs, s, sems):
        for i in range(cuts):
            for j in range(each):
                at = i * each + j
                outs[i][j, :rows] = add_terms(ins.terms, (at, slice(0, rows))).astype(bf16)
                if extra:
                    last = slice(0, extra) if pairs else slice(rows, rows + extra)
                    total = add_pairs(ins.pairs if pairs else ins.terms, (at, last))
                    outs[i][j, rows:] = pair(total)

    return call(
        body,
        Box(terms=list(terms), pairs=list(pairs), token=far(token)),
        [struct((each, rows + extra, D), bf16)] * cuts,
        weight=weight,
        limit=6 * MIB,
    )


def filter_parts(plan, kind, filt, lk, layer):
    if kind == "g":
        return filt[layer, 0], filt[layer, 1]
    return (
        jnp.concatenate([lk[layer, 0]] * plan.group, 0),
        jnp.concatenate([lk[layer, 1]] * plan.group, 0),
    )


def pre_layer(plan, layer, x, vec, filt, lk, tables, n1, s1, spec, n2, s2, u):
    g1, b1, g2, b2 = (vec[i, layer : layer + 1] for i in range(4))
    for seg in plan.segments:
        kind, _, _, row, rows, off, half = seg
        rs = slice(row, row + rows)
        normal, scale = normalize(x[rs])
        n1[rs] = normal
        s1[rs] = scale
        z = normal * g1 + b1
        field = dot(tables.to[kind][...], z, high)
        spec[off : off + 2 * half] = field
        kr, ki = filter_parts(plan, kind, filt, lk, layer)
        re, im = field[:half], field[half:]
        out = jnp.concatenate([re * kr - im * ki, re * ki + im * kr], 0)
        out = out * spectral_weight(plan.grids[kind], 2 * half)
        f = dot(tables.back_to[kind][...], out, high)
        normal, scale = normalize(f)
        n2[rs] = normal
        s2[rs] = scale
        u[rs] = (normal * g2 + b2).astype(bf16)


def pre_layer_back(plan, layer, du, dx, vec, filt, lk, tables, n1, s1, spec, n2, s2, dlk):
    g1, g2 = vec[0, layer : layer + 1], vec[2, layer : layer + 1]
    sums = [jnp.zeros((1, D), f32) for _ in range(4)]
    filt_sum = [jnp.zeros((GSPEC, D), f32) for _ in range(2)]
    local_sum = [jnp.zeros((LSPEC, D), f32) for _ in range(2)]
    for seg in plan.segments:
        kind, _, _, row, rows, off, half = seg
        rs = slice(row, row + rows)
        dout, normal = du[rs], n2[rs]
        sums[2] = sums[2] + jnp.sum(dout * normal, 0, keepdims=True)
        sums[3] = sums[3] + jnp.sum(dout, 0, keepdims=True)
        df = normalize_back(dout, g2, normal, s2[rs])
        grad = dot(tables.to[kind][...], df, high)
        grad = grad * spectral_weight(plan.grids[kind], 2 * half)
        gr, gi = grad[:half], grad[half:]
        re, im = spec[off : off + half], spec[off + half : off + 2 * half]
        kr, ki = filter_parts(plan, kind, filt, lk, layer)
        part_r = gr * re + gi * im
        part_i = gi * re - gr * im
        if kind == "g":
            filt_sum = [filt_sum[0] + part_r, filt_sum[1] + part_i]
        else:
            for i in range(plan.group):
                cut = slice(i * LSPEC, (i + 1) * LSPEC)
                local_sum = [local_sum[0] + part_r[cut], local_sum[1] + part_i[cut]]
        back = jnp.concatenate([gr * kr + gi * ki, gi * kr - gr * ki], 0)
        dz = dot(tables.back_to[kind][...], back, high)
        normal = n1[rs]
        sums[0] = sums[0] + jnp.sum(dz * normal, 0, keepdims=True)
        sums[1] = sums[1] + jnp.sum(dz, 0, keepdims=True)
        dx[rs] = dx[rs] + normalize_back(dz, g1, normal, s1[rs])
    for c in range(2):
        filt_sum[c] = filt_sum[c] + lax.dot_general(
            dlk[...],
            local_sum[c],
            (((0,), (0,)), ((), ())),
            preferred_element_type=f32,
            precision=high,
        )
    return sums, filt_sum


def place_blocks(net, me, pieces, shard, cols, both, sem):
    for array, masks in pieces:
        for j, mask in enumerate(masks):
            d, t = net.place(me, mask)
            rows_at = pl.ds(pl.multiple_of(d * shard, 16), shard)
            cols_at = pl.ds(pl.multiple_of(t * cols, 128), cols)
            for i, matrix in enumerate(both):
                start_copy(
                    array.at[j, pl.ds(i * shard, shard)], matrix.at[rows_at, cols_at], sem.at[i]
                )


def cut_blocks(net, me, shard, cols, both, outs, sem):
    unit = len(net.masks(1))
    for i, mask in enumerate(net.masks(0)):
        d, t = net.place(me, mask)
        rows_at = pl.ds(pl.multiple_of(d * shard, 16), shard)
        cols_at = pl.ds(pl.multiple_of(t * cols, 128), cols)
        for k, matrix in enumerate(both):
            start_copy(
                matrix.at[rows_at, cols_at],
                outs[i // unit].at[i % unit, pl.ds(k * shard, shard)],
                sem.at[k],
            )


def cut_adam(net, me, share, adam, outs):
    unit = len(net.masks(1))
    for i, mask in enumerate(net.masks(0)):
        own = pl.ds(pl.multiple_of((me ^ mask) * share, 8), share)
        outs[i // unit][i % unit] = pair(adam[own, :])


def gelu_parts(a):
    bell = jnp.exp(-0.5 * a * a)
    t = pl.reciprocal(1.0 + (0.3275911 * 0.7071067811865476) * jnp.abs(a))
    tail = 0.5 * 1.061405429 * t - 0.5 * 1.453152027
    for coefficient in (1.421413741, -0.284496736, 0.254829592):
        tail = tail * t + 0.5 * coefficient
    tail = tail * t * bell
    phi = jnp.where(a >= 0.0, 1.0 - tail, tail)
    return a * phi, phi + (a * bell) * 0.3989422804014327


def ff_forward(layer, u, up_s, dn_s, bias, h, gp, acc):
    tiles = [slice(j, j + TILE) for j in range(0, FF, TILE)]

    def first(cols):
        return dot(u[...], up_s[:, cols]) + bias[layer : layer + 1, cols]

    ahead = first(tiles[0])
    for j, cols in enumerate(tiles):
        a = ahead
        if j + 1 < len(tiles):
            ahead = first(tiles[j + 1])
        act, slope = gelu_parts(a)
        act = act.astype(bf16)
        h[:, cols] = act
        gp[:, cols] = slope
        term = dot_last(act, dn_s[:, cols])
        acc[...] = term if j == 0 else acc[...] + term


def ff_backward(dm, h, gp, up_s, dn_s, dbias, du, weights):
    tiles = [slice(j, j + TILE) for j in range(0, FF, TILE)]

    def first(cols):
        return dot(dm[...], dn_s[:, cols])

    ahead = first(tiles[0])
    for j, cols in enumerate(tiles):
        grad = ahead
        if j + 1 < len(tiles):
            ahead = first(tiles[j + 1])
        dpre = (grad * gp[:, cols]).astype(bf16)
        weights(cols, dpre)
        dbias[:, cols] = jnp.sum(dpre.astype(f32), 0, keepdims=True)
        term = dot_last(dpre, up_s[:, cols])
        du[...] = term if j == 0 else du[...] + term


def adam_update(weight, grad, first, second):
    first_new = adam_one * first + (1.0 - adam_one) * grad
    second_new = adam_two * second + (1.0 - adam_two) * grad * grad
    first_hat = first_new / (1.0 - adam_one**STEP)
    second_hat = second_new / (1.0 - adam_two**STEP)
    weight_new = weight * (1.0 - adam_rate * adam_decay) - adam_rate * first_hat / (
        jnp.sqrt(second_hat) + adam_floor
    )
    return (first_new, second_new, weight_new)


def flip(v):
    return v.astype(f32).T.astype(bf16)


def per_device(
    global_tokens,
    local_tokens,
    global_cotangent,
    local_cotangent,
    up_weight,
    down_weight,
    filters,
    resize,
    vectors,
    hidden_bias,
    up_momentum,
    down_momentum,
    filter_means,
    filter_squares,
    vector_means,
    vector_squares,
    bias_means,
    bias_squares,
):
    both = ("dp", "tensor")
    net = Net(lax.axis_size("dp"), lax.axis_size("tensor"))
    parts, across, devices = net.parts, net.across, net.devices
    micro, global_images = global_tokens.shape[:2]
    local_images = local_tokens.shape[1]
    layers, shard, cols = up_weight.shape
    direct = net.power and shard % 16 == 0 and cols == D
    plan = Plan(micro, global_images, local_images)
    rows, spec_rows = plan.rows, plan.spec
    to_tables = {k: jnp.asarray(t) for k, t in plan.tables.items()}
    filt = filters.reshape(layers, 2, GSPEC, D)
    down_t = jnp.swapaxes(down_weight, 1, 2)
    down_momentum_t = jnp.swapaxes(down_momentum, 1, 2)
    vec = jnp.swapaxes(vectors, 0, 1)
    vec_at = 2 * GSPEC
    bias_at = vec_at + 5
    adam_used = bias_at + FF // D
    share = round_up((adam_used + devices - 1) // devices, 8)
    adam_rows = devices * share if direct else round_up(adam_used, 8)
    matrix = struct((D, FF), bf16)
    row_f32 = struct((rows, D), f32)
    row_bf16 = struct((rows, D), bf16)
    column = struct((rows, 1), f32)
    flat = struct((D, rows), bf16)
    hidden = struct((rows, FF), bf16)
    hidden_f32 = struct((rows, FF), f32)
    unit = len(net.masks(1))
    inner = net.masks(2)
    inner1 = inner

    def piece_masks(inside):
        unit_at, size = net.stages[1]
        return [[c + i * unit_at + m for m in inside] for c in range(2) for i in range(size)]

    def whole(got):
        got = got.reshape(parts, across, -1, shard, cols)
        return got.transpose(2, 0, 3, 1, 4).reshape(got.shape[2], D, FF)

    def hold(current, token):
        return gate([current], token)[0] if direct else current

    def gather_near(current, later=None):
        if not direct:
            return far(whole(lax.all_gather(current.reshape(1, -1, cols), both, axis=0, tiled=True)))
        pieces = net.gather_plane(current)
        if later is not None:
            pieces = list(gate(pieces, later))
        return far(net.gather_core(pieces))

    def unpack(operand, inside, matrices, sem):
        if direct:
            pieces = list(zip(operand, piece_masks(inside)))
            place_blocks(net, net.me(), pieces, shard, cols, matrices, sem)
        else:
            for i, m in enumerate(matrices):
                start_copy(operand.at[i], m, sem.at[i])

    def arrived(matrices, sem):
        for i, m in enumerate(matrices):
            wait_copy(m, sem.at[i])

    def give(ins, matrices, outs, sem):
        if direct:
            cut_blocks(net, net.me(), shard, cols, matrices, outs, sem)
        else:
            for i, m in enumerate(matrices):
                start_copy(m, outs[i], sem.at[i])

    grad_shapes = [struct((unit, 2 * shard, D), bf16)] * 2 if direct else [matrix] * 2
    saved_shapes = Box(
        n1=row_f32, s1=column, spec=struct((spec_rows, D), f32), n2=row_f32, s2=column, u=row_bf16
    )
    norm_names = ("n1", "s1", "spec", "n2", "s2")
    chunk_shape = struct((1, 2 * shard, cols), bf16)

    def cast_body(ins, outs, s, sems):
        names = ("up", "dn")
        for i, name in enumerate(names):
            start_copy(ins[name], s[name], sems.given.at[i])
        for i, name in enumerate(names):
            wait_copy(s[name], sems.given.at[i])
            for layer, out in enumerate(outs.chunks):
                out[0, i * shard : (i + 1) * shard] = s[name][layer].astype(bf16)

    block_shape = struct((layers, shard, cols), f32)
    low_weights = call(
        cast_body,
        far(Box(up=up_weight, dn=down_t)),
        Box(chunks=[chunk_shape] * layers),
        Box(up=block_shape, dn=block_shape),
        Box(given=2),
        limit=8 * MIB,
    )
    reached = list(low_weights.chunks)
    if direct:
        reached[0] = net.gather_far(reached[0])
        reached[1], inner1 = net.gather_bits(gate([reached[1]], reached[0])[0])

    def pre_body(ins, outs, s, sems):
        for layer in range(layers):
            for c in range(2):
                outs.lk[layer, c] = dot(ins.resize[...], ins.filt[layer, c], high)
        for seg in plan.segments:
            load_rows(plan, seg, outs.x, ins.gt, ins.lt)
            load_rows(plan, seg, outs.dx, ins.gc, ins.lc)
        for kind, table in ins.to.items():
            outs.back_to[kind][...] = table[...].T
        tables = Box(to=ins.to, back_to=outs.back_to)
        pre_layer(plan, 0, outs.x, ins.vec, ins.filt, outs.lk, tables, **outs.saved)

    pre = call(
        pre_body,
        Box(
            gt=global_tokens, lt=local_tokens, gc=global_cotangent, lc=local_cotangent, vec=vec,
            filt=filt, resize=resize, to=to_tables,
        ),
        Box(
            x=row_f32, dx=row_f32, lk=struct((layers, 2, LSPEC, D), f32), saved=saved_shapes,
            back_to={k: struct(t.shape[::-1], f32) for k, t in to_tables.items()},
        ),
        weight=6,
        limit=10 * MIB,
    )
    saved0, lk = pre.saved, pre.lk
    tables = Box(to=to_tables, back_to=pre.back_to)
    if direct:
        reached[1] = gate([reached[1]], lk)[0]
    weights0 = gather_near(reached[0], reached[1])
    reached1 = hold(reached[1], weights0[len(weights0) // 2 - 1].array) if direct else reached[1]

    def first_body(ins, outs, s, sems):
        unpack(ins.w, inner, outs.w, sems.w)
        arrived(outs.w, sems.w)
        ff_forward(0, ins.u, *outs.w, ins.bias, outs.h, outs.gp, s.acc)
        outs.x[...] = ins.x[...] + s.acc[...] + ins.vec[4, 0:1]

    first = call(
        first_body,
        Box(
            w=weights0, x=pre.x, u=saved0.u, vec=vec, bias=hidden_bias,
            token=far(reached1),
        ),
        Box(h=hidden, gp=hidden_f32, w=[matrix] * 2, x=row_f32),
        Box(acc=row_f32),
        Box(w=2),
        weight=9,
        limit=16 * MIB,
    )
    weights1 = gather_near(reached1, first.x)

    def middle_body(ins, outs, s, sems):
        pre_layer(plan, 1, ins.x, ins.vec, ins.filt, ins.lk, ins.tables, **outs)

    saved1 = call(
        middle_body,
        Box(x=first.x, vec=vec, filt=filt, lk=lk, tables=tables),
        saved_shapes,
        weight=4,
        limit=10 * MIB,
    )

    backward_scratch = Box(grads=[matrix] * 2, dmt=flat, ut=flat)

    def weight_gradients(s, grad, u, h):
        s.dmt[...] = grad.astype(f32).T.astype(bf16)
        s.ut[...] = flip(u[...])

        def tile(cols, dpre):
            s.grads[1][:, cols] = dot(s.dmt[...], h[:, cols]).astype(bf16)
            s.grads[0][:, cols] = dot(s.ut[...], dpre).astype(bf16)

        return tile

    def norms_back(layer, ins, du, dx, saved, tables_ref, shift, dbias, adam, out):
        sums, filt_sum = pre_layer_back(
            plan, layer, du, dx, ins.vec, ins.filt, ins.lk, tables_ref,
            dlk=ins.resize, **{k: saved[k] for k in norm_names},
        )
        for c in range(2):
            adam[c * GSPEC : (c + 1) * GSPEC] = filt_sum[c]
        for i in range(4):
            adam[vec_at + i : vec_at + i + 1] = sums[i]
        adam[vec_at + 4 : vec_at + 5] = shift[...]
        for i in range(FF // D):
            adam[bias_at + i : bias_at + i + 1] = dbias[:, i * D : (i + 1) * D]
        if adam_rows > adam_used:
            adam[adam_used:] = jnp.zeros((adam_rows - adam_used, D), f32)
        if direct:
            cut_adam(net, net.me(), share, adam, out)
        else:
            out[0][...] = adam[...]

    adam_shape = struct((adam_rows, D), f32)
    adam_shapes = [struct((unit, 2 * share, D), bf16)] * 2 if direct else [adam_shape]
    line = struct((1, D), f32)
    wide_line = struct((1, FF), f32)

    def second_body(ins, outs, s, sems):
        saved = ins.saved
        unpack(ins.w, inner1, s.w, sems.w)
        arrived(s.w, sems.w)
        ff_forward(1, saved.u, *s.w, ins.bias, s.h, s.gp, s.acc)
        outs.y[...] = ins.x[...] + s.acc[...] + ins.vec[4, 1:2]
        grad = ins.dx[...].astype(bf16)
        s.dm[...] = grad
        outs.shift[...] = jnp.sum(grad.astype(f32), 0, keepdims=True)
        tile = weight_gradients(s, grad, saved.u, s.h)
        ff_backward(s.dm, s.h, s.gp, *s.w, outs.dbias, outs.du, tile)
        give(ins, s.grads, outs.grads, sems.taken)
        arrived(s.grads, sems.taken)

    second = call(
        second_body,
        Box(w=weights1, x=first.x, saved=saved1, vec=vec, bias=hidden_bias, dx=pre.dx),
        Box(
            y=row_f32,
            grads=far(grad_shapes),
            du=row_f32,
            dbias=wide_line,
            shift=line,
        ),
        Box(acc=row_f32, h=hidden, gp=hidden_f32, w=[matrix] * 2, dm=row_bf16, **backward_scratch),
        Box(w=2, taken=2),
        weight=14,
        limit=25 * MIB,
    )

    def branch_body(ins, outs, s, sems):
        outs.dx[...] = ins.dx[...]
        norms_back(
            1, ins, ins.du, outs.dx, ins.saved, ins.tables, ins.shift, ins.dbias, s.adam, outs.adam
        )

    branch = call(
        branch_body,
        Box(
            du=second.du, dx=pre.dx, saved=saved1, shift=second.shift, dbias=second.dbias, vec=vec,
            filt=filt, lk=lk, resize=resize, tables=tables,
        ),
        Box(dx=row_f32, adam=adam_shapes),
        Box(adam=adam_shape),
        weight=3,
        limit=12 * MIB,
    )
    if direct:
        terms1 = net.exchange(0, second.grads)
        pairs1 = net.exchange(0, branch.adam)
        terms1 = sum_stage(terms1, pairs1, net.stages[1][1])
    else:
        terms1 = second.grads

    def third_body(ins, outs, s, sems):
        grad = ins.dx[...].astype(bf16)
        s.dm[...] = grad
        outs.shift[...] = jnp.sum(grad.astype(f32), 0, keepdims=True)
        tile = weight_gradients(s, grad, ins.u, ins.h)
        ff_backward(
            s.dm, ins.h, ins.gp, *ins.w, outs.dbias, outs.du, tile
        )
        give(ins, s.grads, outs.grads, sems.taken)
        arrived(s.grads, sems.taken)

    third = call(
        third_body,
        Box(
            w=first.w, dx=branch.dx, u=saved0.u, h=first.h, gp=first.gp, token=far(terms1[0])
        ),
        Box(grads=far(grad_shapes), du=row_f32, dbias=wide_line, shift=line),
        Box(dm=row_bf16, **backward_scratch),
        Box(taken=2),
        limit=12 * MIB,
    )
    grads0 = third.grads
    def fourth_body(ins, outs, s, sems):
        s.dx[...] = ins.dx[...]
        norms_back(
            0, ins, ins.du, s.dx, ins.saved, ins.tables, ins.shift,
            ins.dbias, s.adam, outs.adam,
        )
        for seg in plan.segments:
            store_rows(plan, seg, s.dx, outs.ggrad, outs.lgrad, False)
            store_rows(plan, seg, ins.y, outs.gout, outs.lout, True)

    fourth = call(
        fourth_body,
        Box(
            y=second.y,
            dx=branch.dx, du=third.du, dbias=third.dbias, shift=third.shift,
            saved={k: saved0[k] for k in norm_names}, vec=vec, filt=filt, lk=lk,
            resize=resize, tables=tables, token=far(terms1[0]),
        ),
        Box(
            gout=struct((global_images, TOKG, micro, D), bf16),
            lout=struct((micro, TOKL, local_images, D), bf16),
            ggrad=struct((micro, TOKG, global_images, D), f32),
            lgrad=struct((micro, TOKL, local_images, D), f32),
            adam=adam_shapes,
        ),
        Box(dx=row_f32, adam=adam_shape),
        limit=10 * MIB,
    )

    block = struct((shard, cols), f32)

    def momentum(layer, terms, token=(), others=None):
        if not direct:
            terms = jnp.stack(terms).reshape(2, parts, shard, across, cols)
            terms = terms.transpose(1, 3, 0, 2, 4).reshape(devices * 2, shard, cols)
            mine = lax.psum_scatter(terms, both, scatter_dimension=0, tiled=True).astype(f32)
            up = momentum_decay * up_momentum[layer] + mine[0]
            dn = momentum_decay * down_momentum_t[layer] + mine[1]
            return Box(up=up, dn=dn, chunk=jnp.concatenate([up, dn], 0).astype(bf16)[None])
        chunk = terms[0].shape[1]

        def body(ins, outs, s, sems):
            for i, name in enumerate(("up", "dn")):
                at = slice(i * shard, (i + 1) * shard)
                velocity = momentum_decay * ins[name][layer] + add_terms(ins.terms, (0, at))
                if others is None:
                    outs[name][...] = velocity
                else:
                    outs[name][layer] = velocity
                    outs[name][1 - layer] = ins.others[i][...]
                outs.chunk[0, at] = velocity.astype(bf16)
            outs.chunk[0, 2 * shard :] = pair(
                add_pairs(ins.terms, (0, slice(2 * shard, chunk)))
            )

        shape = block if others is None else block_shape
        return call(
            body,
            Box(
                terms=terms, up=up_momentum, dn=down_momentum_t, token=far(token),
                others=() if others is None else others,
            ),
            Box(up=shape, dn=shape, chunk=struct((1, chunk, D), bf16)),
            weight=0 if others is None else 20,
            limit=8 * MIB,
        )

    shown = [jnp.transpose(fourth.gout, (2, 0, 1, 3))] + [
        jnp.swapaxes(a, 1, 2) for a in (fourth.lout, fourth.ggrad, fourth.lgrad)
    ]
    if direct:
        cuts = [size for _, size in net.stages] + [1]
        terms1 = sum_stage(net.exchange(1, terms1), (), cuts[2], 2 * share, (), 20)
        terms0, pairs0 = net.exchange(0, grads0), net.exchange(0, fourth.adam)
        terms0 = sum_stage(terms0, pairs0, cuts[1], token=terms1[0])
        next0 = net.exchange(1, terms0)
        if len(net.stages) == 3:
            new1 = momentum(1, net.exchange(2, terms1), terms0[0])
            terms0 = sum_stage(next0, (), cuts[2], 2 * share, new1.chunk)
        else:
            terms0 = sum_stage(next0, (), cuts[2], 2 * share)
        for index in range(2, len(net.stages)):
            if index + 1 < len(net.stages):
                terms1 = net.exchange(index, terms1)
                terms1 = sum_stage(terms1, (), cuts[index + 1], 2 * share, terms0[0])
                terms0 = net.exchange(index, terms0)
                terms0 = sum_stage(terms0, (), cuts[index + 1], 2 * share, terms1[0])
        if len(net.stages) > 3:
            new1 = momentum(1, net.exchange(len(net.stages) - 1, terms1), terms0[0])
        new0 = momentum(
            0, net.exchange(len(net.stages) - 1, terms0), (), (new1.up, new1.dn)
        )
        reached1, inner1 = net.gather_bits(new1.chunk, (terms0[0], new0.chunk))
        up_velocity, down_velocity = new0.up, new0.dn
    else:
        new1 = momentum(1, terms1)
        new0 = momentum(0, grads0)
        up_velocity, down_velocity = (jnp.stack([new0[k], new1[k]]) for k in ("up", "dn"))

    scale_out = muon_rate * 0.2 * math.sqrt(max(D, FF))

    def eye():
        return (
            lax.broadcasted_iota(jnp.int32, (D, D), 0) == lax.broadcasted_iota(jnp.int32, (D, D), 1)
        ).astype(f32)

    def polynomial(gram, gram_s, poly_s, rows_at):
        one = eye()
        scale = 1.0 / (jnp.sqrt(jnp.sum(gram * one, keepdims=True)) + 1e-07)
        gram = gram * (scale * scale)
        gram_s[...] = gram
        poly_s[...] = ns_a * one + ns_b * gram + ns_c * dot(gram, gram, high)
        chain = [poly_s[rows_at]]
        for _ in range(2):
            row = chain[-1]
            for factor in (poly_s, gram_s, poly_s):
                row = dot(row, factor[...], high)
            chain.append(row)
        return (ns_a * chain[0] + ns_b * chain[1] + ns_c * chain[2]) * scale

    square = struct((D, D), f32)
    old = Box(up=up_weight, dn=down_t)
    names = ("up", "dn")

    def new_weight(old_weight, q_rows, v):
        orth = dot(q_rows, v)
        return old_weight * (1.0 - muon_rate * muon_decay) - scale_out * orth

    adam_ins = Box(
        filt=(filt, filter_means.reshape(filt.shape), filter_squares.reshape(filt.shape)),
        vec=(vec, jnp.swapaxes(vector_means, 0, 1), jnp.swapaxes(vector_squares, 0, 1)),
        bias=(hidden_bias, bias_means, bias_squares),
    )
    adam_shapes_out = jax.tree.map(lambda a: struct(a.shape, f32), adam_ins)
    adam_count = len(jax.tree.leaves(adam_ins))

    def adam_step(ins, outs, name, at, grad):
        old, mean, square = (ref[at] for ref in ins[name])
        for ref, value in zip(outs[name], adam_update(old, grad, mean, square)):
            ref[at] = value

    def adam_lines(ins, outs, layer, rows_at):
        for i in range(5):
            adam_step(ins, outs, "vec", (i, slice(layer, layer + 1)), rows_at(i))
        for i in range(FF // D):
            at = (slice(layer, layer + 1), slice(i * D, (i + 1) * D))
            adam_step(ins, outs, "bias", at, rows_at(5 + i))

    def copies(pairs, sems, action):
        for i, (src, dst) in enumerate(pairs):
            getattr(pltpu.make_async_copy(src, dst, sems.at[i]), action)()

    def muon_whole():
        moved = [
            whole(lax.all_gather(new.chunk[0].reshape(1, -1, cols), both, axis=0, tiled=True))
            for new in (new0, new1)
        ]
        start = lax.axis_index("dp") * shard

        def widen(weight):
            wide = jnp.zeros((layers, D, cols), f32)
            return lax.dynamic_update_slice_in_dim(wide, weight, start, 1)

        def body(ins, outs, s, sems):
            for layer in range(layers):
                total = ins.total.at[layer]
                for c in range(2):
                    rows_in = total[c * GSPEC : (c + 1) * GSPEC]
                    adam_step(ins.adam, outs.adam, "filt", (layer, c), rows_in)
                adam_lines(
                    ins.adam, outs.adam, layer, lambda i: total[vec_at + i : vec_at + i + 1]
                )
            cols_at = pl.ds(pl.multiple_of((net.me() % across) * cols, 128), cols)
            for layer in range(layers):
                for i, name in enumerate(names):
                    v = ins.v[layer][i]
                    q = polynomial(dot_last(v, v), s.gram, s.poly, slice(0, D))
                    part = ins.v[layer][i, :, cols_at]
                    outs[name][layer] = new_weight(ins.old[name][layer], q.astype(bf16), part)

        wide = struct((layers, D, cols), f32)
        last = call(
            body,
            Box(
                v=moved, old={k: widen(v) for k, v in old.items()}, adam=adam_ins,
                total=lax.psum(jnp.stack([fourth.adam[0], branch.adam[0]]), both),
            ),
            Box(up=wide, dn=wide, adam=adam_shapes_out),
            Box(gram=square, poly=square),
            limit=48 * MIB,
        )
        up, dn = (lax.dynamic_slice_in_dim(last[k], start, shard, 1) for k in names)
        return up, dn, last.adam

    def muon_direct():
        core_unit, far_unit = 1, 2
        half = D // 3
        places = [(0, 0), (0, 1), (0, 2), (1, 1), (1, 2), (2, 2)]
        tall = 2 * half
        far_bits = [2**b for b in range(2, net.bits) if 2**b < net.stages[1][0] * net.stages[1][1]]
        column_masks = []
        for masks in (inner, inner1):
            for bit in far_bits:
                masks = masks + [bit + m for m in masks]
            column_masks.append(masks)
        mine_rows = len(column_masks[0]) * share

        def pack(gram, out, start):
            for k, (r, c) in enumerate(places):
                at = pl.ds(start + (k // 3) * half, half)
                block_of = gram[r * half : (r + 1) * half, c * half : (c + 1) * half]
                out[at, (k % 3) * half : (k % 3 + 1) * half] = block_of.astype(bf16)

        def unpack_gram(terms, out):
            for k, (r, c) in enumerate(places):
                at = (pl.ds((k // 3) * half, half), pl.ds((k % 3) * half, half))
                value = terms[0][at].astype(f32) + terms[1][at].astype(f32)
                out[r * half : (r + 1) * half, c * half : (c + 1) * half] = value
                if r != c:
                    out[c * half : (c + 1) * half, r * half : (r + 1) * half] = value.T

        def gram_stage(layer, pieces, token):
            def body(ins, outs, s, sems):
                me_at = net.me()
                index = 0
                for array in ins.pieces:
                    for j in range(array.shape[0]):
                        d, _ = net.place(me_at, column_masks[layer][index])
                        at = pl.ds(pl.multiple_of(d * shard, 16), shard)
                        for i in range(2):
                            outs.v[i, at] = array[j, i * shard : (i + 1) * shard]
                        sums = add_pairs([array], (j, slice(2 * shard, 2 * shard + 2 * share)))
                        s.adam[index * share : (index + 1) * share] = sums
                        index += 1
                for i in range(2):
                    v = outs.v[i]
                    s.gram[i] = dot_last(v, v)
                core = me_at & 1
                pack(s.gram.at[core], outs.keep, 0)
                pack(s.gram.at[1 - core], outs.send, 0)
                rows_out = s.adam[...].astype(bf16)
                outs.send[tall:] = rows_out
                outs.adam[...] = rows_out

            return call(
                body,
                Box(pieces=pieces, token=far(token)),
                Box(
                    v=struct((2, D, cols), bf16),
                    keep=struct((tall, D), bf16),
                    adam=struct((mine_rows, D), bf16),
                    send=struct((tall + mine_rows, D), bf16),
                ),
                Box(gram=struct((2, D, D), f32), adam=struct((mine_rows, D), f32)),
                limit=16 * MIB,
            )

        def core_sum(keep, got, token):
            def body(ins, outs, s, sems):
                keep_ref, got_ref = ins.keep, ins.got
                outs[...] = (keep_ref[...].astype(f32) + got_ref[:tall].astype(f32)).astype(bf16)

            return call(
                body,
                Box(keep=keep, got=got, token=far(token)),
                struct((tall, D), bf16),
                limit=4 * MIB,
            )

        def pick_stage(keep, got, other):
            def body(ins, outs, s, sems):
                keep_ref, got_ref = ins.keep, ins.got
                x = (net.me() >> 1) & 1
                s.both[0] = (
                    keep_ref[...].astype(f32) + got_ref[:tall].astype(f32)
                ).astype(bf16)
                s.both[1] = ins.other[...]
                outs.mine[...] = s.both[x]
                outs.send[...] = s.both[1 - x]

            return call(
                body,
                Box(keep=keep, got=got, other=other),
                Box(mine=struct((tall, D), bf16), send=struct((tall, D), bf16)),
                Box(both=struct((2, tall, D), bf16)),
                limit=4 * MIB,
            )

        def poly_stage(mine, got):
            def body(ins, outs, s, sems):
                unpack_gram((ins.mine, ins.got), s.sum)
                d, _ = net.place(net.me(), 0)
                rows_at = pl.ds(pl.multiple_of(d * shard, 8), shard)
                q = polynomial(s.sum[...], s.gram, s.poly, rows_at)
                outs[...] = q.astype(bf16)

            return call(
                body,
                Box(mine=mine, got=got),
                struct((shard, D), bf16),
                Box(sum=square, gram=square, poly=square),
                weight=3,
                limit=8 * MIB,
            )

        def final_stage(vs, qs):
            def body(ins, outs, s, sems):
                at = net.me() & 3
                for mask, q in enumerate(ins.qs):
                    s.q[at ^ mask] = q[...]
                for layer in range(layers):
                    for i, name in enumerate(names):
                        q_rows = s.q[2 * layer + i]
                        outs[name][layer] = new_weight(
                            ins.old[name][layer], q_rows, ins.vs[layer][i]
                        )

            return call(
                body,
                Box(vs=vs, qs=qs, old=old),
                Box(up=block_shape, dn=block_shape),
                Box(q=struct((4, shard, D), bf16)),
                limit=6 * MIB,
            )

        line_rows = adam_rows - vec_at

        def mark_of(tree, key):
            marks = Box({k: jax.tree.map(lambda _: k == key, v) for k, v in tree.items()})
            return [i for i, mark in enumerate(jax.tree.leaves(marks)) if mark]

        def adam_stage(layer, columns, before, token=()):
            last = before is not None
            kinds = ("vec", "bias") if last else ()

            def body(ins, outs, s, sems):
                filts = [ref.at[layer] for ref in ins.adam.filt]
                filts_out = [ref.at[layer] for ref in outs.filt]
                whole_in = [(r, t) for k in kinds for r, t in zip(ins.adam[k], s.given[k])]
                loads = list(zip(filts, s.given.filt)) + whole_in
                copies(loads, sems.given, "start")
                for number, array in enumerate(ins.columns):
                    first_row = columns[number][1]
                    values = array[first_row : first_row + mine_rows].astype(f32)
                    for i, mask in enumerate(column_masks[layer]):
                        at = (net.me() ^ (mask | number)) * share
                        s.total[pl.ds(pl.multiple_of(at, 8), share)] = values[
                            i * share : (i + 1) * share
                        ]
                copies(loads, sems.given, "wait")
                for c in range(2):
                    grad = s.total[c * GSPEC : (c + 1) * GSPEC]
                    adam_step(s.given, s.taken, "filt", c, grad)
                stores = list(zip(s.taken.filt, filts_out))
                if last:
                    for number, ref, start in ((layer, s.total, vec_at), (1 - layer, ins.lines, 0)):
                        adam_lines(
                            s.given, s.taken, number,
                            lambda i, ref=ref, start=start: ref[start + i : start + i + 1],
                        )
                    stores += [(t, r) for k in kinds for t, r in zip(s.taken[k], outs[k])]
                else:
                    outs.lines[...] = s.total[vec_at:]
                copies(stores, sems.taken, "start")
                copies(stores, sems.taken, "wait")

            part = Box(filt=[struct(filt.shape[1:], f32)] * 3, **{k: adam_shapes_out[k] for k in kinds})
            ins = Box(adam=far(adam_ins), columns=[a for a, _ in columns], token=far(token))
            outs = Box(filt=far(list(adam_shapes_out.filt)))
            aliases = None
            if last:
                outs.update({k: far(adam_shapes_out[k]) for k in kinds})
                ins.lines = before.lines
                ins.done = far(before.filt)
                marks = mark_of(ins, "done")
                aliases = dict(zip(marks, mark_of(outs, "filt")))
            else:
                outs.lines = struct((line_rows, D), f32)
            count = 3 + 3 * len(kinds)
            return call(
                body,
                ins,
                outs,
                Box(given=part, taken=part, total=struct((adam_rows, D), f32)),
                Box(given=count, taken=count),
                weight=2,
                limit=8 * MIB,
                aliases=aliases,
            )

        def column(array):
            pieces = [array]
            for bit in far_bits:
                pieces = pieces + [net.swap(p, bit) for p in pieces]
            return pieces

        reached0 = net.gather_far(new0.chunk)
        gram1 = gram_stage(1, column(reached1), reached0)
        far1 = [net.swap(gram1.adam, mask) for mask in (2, 3)]
        gram0 = gram_stage(0, column(reached0), far1)
        got1, got0 = (net.swap(gram.send, core_unit) for gram in (gram1, gram0))
        rows1 = [(gram1.adam, 0), (got1, tall)] + [(a, 0) for a in far1]
        sum1 = core_sum(gram1.keep, got1, gram0.keep)
        picked = pick_stage(gram0.keep, got0, sum1)
        adam1 = adam_stage(1, rows1, None, picked.mine)
        q = poly_stage(picked.mine, net.swap(picked.send, far_unit))
        (late,) = gate([gram0.adam], adam1.lines)
        rows0 = [(late, 0), (got0, tall)] + [(net.swap(late, mask), 0) for mask in (2, 3)]
        adam_outs = adam_stage(0, rows0, adam1)
        qs = [q] + [net.swap(q, mask) for mask in (1, 2, 3)]
        final = final_stage([gram0.v, gram1.v], qs)
        return final.up, final.dn, adam_outs

    if direct:
        up_master, down_master, adam_outs = muon_direct()
    else:
        up_master, down_master, adam_outs = muon_whole()
    filter_mean, filter_square, filter_master = (
        a.reshape(filters.shape) for a in adam_outs.filt
    )
    vector_mean, vector_square, vector_master = (
        jnp.swapaxes(a, 0, 1) for a in adam_outs.vec
    )
    bias_mean, bias_square, bias_master = adam_outs.bias
    return (
        *shown,
        up_velocity,
        up_master,
        jnp.swapaxes(down_velocity, 1, 2),
        jnp.swapaxes(down_master, 1, 2),
        filter_mean,
        filter_square,
        filter_master,
        vector_mean,
        vector_square,
        vector_master,
        bias_mean,
        bias_square,
        bias_master,
    )


def solution(mesh):
    images = P(None, ("dp", "tensor"), None, None)
    up, down = P(None, "dp", "tensor"), P(None, "tensor", "dp")
    in_specs = (images,) * 4 + (up, down) + (P(),) * 4 + (up, down) + (P(),) * 6
    out_specs = (images,) * 4 + (up, up, down, down) + (P(),) * 9
    return jax.shard_map(
        per_device, mesh=mesh, in_specs=in_specs, out_specs=out_specs, check_vma=False
    )
```

```python
import math

import jax
import jax.numpy as jnp
import numpy as np
from jax import lax
from jax.experimental import pallas as pl
from jax.experimental.pallas import tpu as pltpu
from jax.sharding import PartitionSpec as P

D = 384
FF = 1536
GRID = 14
LGRID = 6
TOKG = GRID * GRID
TOKL = LGRID * LGRID
GSPEC = 112
LSPEC = 24
STEP = 5
TILE = 256
SCALE = 1.15e9
MIB = 1024 * 1024

high = lax.Precision.HIGH
epsilon_norm = 1e-06
ns_a = 3.4445
ns_b = -4.775
ns_c = 2.0315
momentum_decay = 0.95
muon_rate = 0.25
muon_decay = 0.01
adam_one = 0.9
adam_two = 0.95
adam_rate = 0.25
adam_decay = 0.01
adam_floor = 1e-08
contract_last = (((1,), (1,)), ((), ()))
f32 = jnp.float32
bf16 = jnp.bfloat16


def round_up(value, unit):
    return (value + unit - 1) // unit * unit


def dft_table(grid, copies, rows):
    freq_count = grid // 2 + 1
    spec = np.arange(grid * freq_count)
    cell = np.arange(grid * grid)
    phase = (
        np.outer(spec // freq_count, cell // grid) + np.outer(spec % freq_count, cell % grid)
    ) % grid
    theta = 2.0 * np.pi / grid * phase
    eye = np.eye(copies)
    table = np.concatenate([np.kron(eye, np.cos(theta)), np.kron(eye, -np.sin(theta))], 0)
    return np.pad(table, ((0, 0), (0, rows - table.shape[1]))).astype(np.float32)


def spectral_weight(grid, rows):
    freq_count = grid // 2 + 1
    second = lax.rem(lax.broadcasted_iota(jnp.int32, (rows, D), 0), jnp.int32(freq_count))
    once = (second == 0) | (2 * second == grid)
    return jnp.where(once, 1.0, 2.0).astype(f32) / (grid * grid)


class Plan:
    def __init__(self, micro, global_images, local_images):
        self.micro = micro
        self.group = 4 if local_images % 4 == 0 else local_images
        self.g_rows = round_up(TOKG, 16)
        self.l_rows = round_up(self.group * TOKL, 16)
        self.segments = []
        row = spec = 0
        for m in range(micro):
            for image in range(global_images):
                self.segments.append(("g", m, image, row, self.g_rows, spec, GSPEC))
                row += self.g_rows
                spec += 2 * GSPEC
            for image in range(0, local_images, self.group):
                half = self.group * LSPEC
                self.segments.append(("l", m, image, row, self.l_rows, spec, half))
                row += self.l_rows
                spec += 2 * half
        self.rows = row
        self.spec = spec
        self.tables = {
            "g": dft_table(GRID, 1, self.g_rows), "l": dft_table(LGRID, self.group, self.l_rows)
        }
        self.grids = {"g": GRID, "l": LGRID}


def dot(a, b, precision=None):
    return jnp.dot(a, b, preferred_element_type=f32, precision=precision)


def dot_last(a, b):
    return lax.dot_general(a, b, contract_last, preferred_element_type=f32)


def load_rows(plan, seg, dst, g_ref, l_ref):
    kind, m, image, row, rows, _, _ = seg
    if kind == "g":
        if rows != TOKG:
            start = TOKG // 8 * 8
            dst[row + start : row + rows] = jnp.zeros((rows - start, D), f32)
        dst[row : row + TOKG] = g_ref[m, image].astype(f32)
    else:
        used = plan.group * TOKL
        if rows != used:
            start = used // 8 * 8
            dst[row + start : row + rows] = jnp.zeros((rows - start, D), f32)
        for i in range(plan.group):
            dst[row + i * TOKL : row + (i + 1) * TOKL] = l_ref[m, image + i].astype(f32)


def store_rows(plan, seg, src, g_ref, l_ref, micro_inner):
    kind, m, image, row, _, _, _ = seg
    if kind == "g":
        value = src[row : row + TOKG].astype(g_ref.dtype)
        if micro_inner:
            g_ref[image, :, m, :] = value
        else:
            g_ref[m, :, image, :] = value
    else:
        for i in range(plan.group):
            value = src[row + i * TOKL : row + (i + 1) * TOKL].astype(l_ref.dtype)
            l_ref[m, :, image + i, :] = value


def normalize(v):
    center = v - jnp.mean(v, -1, keepdims=True)
    scale = lax.rsqrt(jnp.mean(center * center, -1, keepdims=True) + epsilon_norm)
    return center * scale, scale


def normalize_back(dout, gain, normal, scale):
    dn = dout * gain
    return scale * (
        dn
        - jnp.mean(dn, -1, keepdims=True)
        - normal * jnp.mean(dn * normal, -1, keepdims=True)
    )


@jax.tree_util.register_pytree_node_class
class Box(dict):
    __getattr__ = dict.__getitem__
    __setattr__ = dict.__setitem__

    def tree_flatten(self):
        keys = tuple(sorted(self))
        return [self[k] for k in keys], keys

    @classmethod
    def tree_unflatten(cls, keys, values):
        return cls(zip(keys, values))


def struct(shape, dtype):
    return jax.ShapeDtypeStruct(shape, dtype)


class Far:
    def __init__(self, array):
        self.array = array


def far(tree):
    return jax.tree.map(Far, tree)


def call(body, ins, outs, scratch=None, sems=None, weight=0, limit=32 * MIB, aliases=None):
    scratch = {} if scratch is None else scratch
    sems = {} if sems is None else sems
    in_leaves, in_tree = jax.tree.flatten(ins)
    out_leaves, out_tree = jax.tree.flatten(outs)
    scratch_leaves, scratch_tree = jax.tree.flatten(scratch)
    sem_leaves, sem_tree = jax.tree.flatten(sems)

    def kernel(*refs):
        cuts = np.cumsum([len(in_leaves), len(out_leaves), len(scratch_leaves)])
        parts = [refs[: cuts[0]], refs[cuts[0] : cuts[1]], refs[cuts[1] : cuts[2]], refs[cuts[2] :]]
        trees = [in_tree, out_tree, scratch_tree, sem_tree]
        body(*(jax.tree.unflatten(t, p) for t, p in zip(trees, parts)))

    def spec(leaf):
        if isinstance(leaf, Far):
            return pl.BlockSpec(memory_space=pl.ANY)
        return pl.BlockSpec(memory_space=pltpu.SMEM if leaf.dtype == jnp.int32 else pltpu.VMEM)

    def plain(leaf):
        return leaf.array if isinstance(leaf, Far) else leaf

    total = sum(
        math.prod(plain(a).shape) * plain(a).dtype.itemsize for a in in_leaves + out_leaves
    )
    result = pl.pallas_call(
        kernel,
        out_shape=[plain(a) for a in out_leaves],
        in_specs=[spec(a) for a in in_leaves],
        out_specs=[spec(a) for a in out_leaves],
        scratch_shapes=[pltpu.VMEM(a.shape, a.dtype) for a in scratch_leaves]
        + [pltpu.SemaphoreType.DMA((n,)) for n in sem_leaves],
        input_output_aliases={} if aliases is None else aliases,
        compiler_params=pltpu.CompilerParams(vmem_limit_bytes=limit),
        cost_estimate=pl.CostEstimate(
            flops=int(weight * SCALE), bytes_accessed=total if weight else 0, transcendentals=0
        ),
    )(*(plain(a) for a in in_leaves))
    return jax.tree.unflatten(out_tree, result)


def gate(arrays, token):
    count = len(arrays)
    return pl.pallas_call(
        lambda *refs: None,
        out_shape=[struct(a.shape, a.dtype) for a in arrays],
        in_specs=[pl.BlockSpec(memory_space=pl.ANY)] * (count + 1),
        out_specs=[pl.BlockSpec(memory_space=pl.ANY)] * count,
        input_output_aliases={i: i for i in range(count)},
        compiler_params=pltpu.CompilerParams(vmem_limit_bytes=MIB),
    )(*arrays, token)


def start_copy(src, dst, sem):
    pltpu.make_async_copy(src, dst, sem).start()


def wait_copy(like, sem):
    pltpu.make_async_copy(like, like, sem).wait()


def join(arrays, token=()):
    each, rows, _ = arrays[0].shape

    def body(ins, outs, s, sems):
        for i, array in enumerate(ins.arrays):
            for j in range(each):
                outs[i * each + j] = array[j]

    shape = struct((each * len(arrays), rows, D), bf16)
    return call(body, Box(arrays=arrays, token=far(token)), shape, limit=8 * MIB)


class Net:
    def __init__(self, parts, across):
        self.parts, self.across = parts, across
        self.devices = parts * across
        self.bits = self.devices.bit_length() - 1
        self.power = 2**self.bits == self.devices
        self.stages = [(1, 2)]
        bit = 1
        while bit < self.bits:
            width = min(2, self.bits - bit)
            self.stages.append((2**bit, 2**width))
            bit += width

    def me(self):
        return lax.axis_index("dp") * self.across + lax.axis_index("tensor")

    def swap(self, array, mask):
        pairs = [(i, i ^ mask) for i in range(self.devices)]
        return lax.ppermute(array, ("dp", "tensor"), pairs)

    def masks(self, first):
        found = [0]
        for unit, size in reversed(self.stages[first:]):
            found = [i * unit + m for i in range(size) for m in found]
        return found

    def place(self, me, mask):
        other = me ^ mask
        return other >> (self.across.bit_length() - 1), other & (self.across - 1)

    def stack(self, array, index, token=()):
        unit, size = self.stages[index]
        return join([array] + [self.swap(array, i * unit) for i in range(1, size)], token)

    def gather_far(self, chunk, token=()):
        for index in reversed(range(2, len(self.stages))):
            chunk = self.stack(chunk, index, token)
        return chunk

    def gather_bits(self, chunk, tokens=((), ())):
        masks = [0]
        first = self.stages[1][0] * self.stages[1][1]
        bits = [b for b in range(self.bits) if 2**b >= first]
        for bit in reversed(bits):
            token = tokens[1] if bit == bits[0] else tokens[0] if bit == bits[-1] else ()
            chunk = join([chunk, self.swap(chunk, 2**bit)], token)
            masks = masks + [2**bit + m for m in masks]
        return chunk, masks

    def gather_plane(self, current):
        unit, size = self.stages[1]
        return [current] + [self.swap(current, i * unit) for i in range(1, size)]

    def gather_core(self, pieces):
        return pieces + [self.swap(array, 1) for array in pieces]

    def exchange(self, index, arrays):
        unit, size = self.stages[index]
        return [arrays[0]] + [self.swap(arrays[i], i * unit) for i in range(1, size)]


def add_terms(terms, at):
    total = terms[0][at].astype(f32)
    for term in terms[1:]:
        total = total + term[at].astype(f32)
    return total


def pair(total):
    first = total.astype(bf16).astype(f32)
    return jnp.concatenate([first, total - first], 0).astype(bf16)


def add_pairs(terms, at):
    total = add_terms(terms, at)
    half = total.shape[0] // 2
    return total[:half] + total[half:]


def sum_stage(terms, pairs, cuts, pairs_in=0, token=(), weight=0):
    count, rows, _ = terms[0].shape
    rows -= pairs_in
    each = count // cuts
    extra = pairs[0].shape[1] if pairs else pairs_in

    def body(ins, outs, s, sems):
        for i in range(cuts):
            for j in range(each):
                at = i * each + j
                outs[i][j, :rows] = add_terms(ins.terms, (at, slice(0, rows))).astype(bf16)
                if extra:
                    last = slice(0, extra) if pairs else slice(rows, rows + extra)
                    total = add_pairs(ins.pairs if pairs else ins.terms, (at, last))
                    outs[i][j, rows:] = pair(total)

    return call(
        body,
        Box(terms=list(terms), pairs=list(pairs), token=far(token)),
        [struct((each, rows + extra, D), bf16)] * cuts,
        weight=weight,
        limit=6 * MIB,
    )


def filter_parts(plan, kind, filt, lk, layer):
    if kind == "g":
        return filt[layer, 0], filt[layer, 1]
    return (
        jnp.concatenate([lk[layer, 0]] * plan.group, 0),
        jnp.concatenate([lk[layer, 1]] * plan.group, 0),
    )


def pre_layer(plan, layer, x, vec, filt, lk, tables, n1, s1, spec, n2, s2, u):
    g1, b1, g2, b2 = (vec[i, layer : layer + 1] for i in range(4))
    for seg in plan.segments:
        kind, _, _, row, rows, off, half = seg
        rs = slice(row, row + rows)
        normal, scale = normalize(x[rs])
        n1[rs] = normal
        s1[rs] = scale
        z = normal * g1 + b1
        field = dot(tables.to[kind][...], z, high)
        spec[off : off + 2 * half] = field
        kr, ki = filter_parts(plan, kind, filt, lk, layer)
        re, im = field[:half], field[half:]
        out = jnp.concatenate([re * kr - im * ki, re * ki + im * kr], 0)
        out = out * spectral_weight(plan.grids[kind], 2 * half)
        f = dot(tables.back_to[kind][...], out, high)
        normal, scale = normalize(f)
        n2[rs] = normal
        s2[rs] = scale
        u[rs] = (normal * g2 + b2).astype(bf16)


def pre_layer_back(plan, layer, du, dx, vec, filt, lk, tables, n1, s1, spec, n2, s2, dlk):
    g1, g2 = vec[0, layer : layer + 1], vec[2, layer : layer + 1]
    sums = [jnp.zeros((1, D), f32) for _ in range(4)]
    filt_sum = [jnp.zeros((GSPEC, D), f32) for _ in range(2)]
    local_sum = [jnp.zeros((LSPEC, D), f32) for _ in range(2)]
    for seg in plan.segments:
        kind, _, _, row, rows, off, half = seg
        rs = slice(row, row + rows)
        dout, normal = du[rs], n2[rs]
        sums[2] = sums[2] + jnp.sum(dout * normal, 0, keepdims=True)
        sums[3] = sums[3] + jnp.sum(dout, 0, keepdims=True)
        df = normalize_back(dout, g2, normal, s2[rs])
        grad = dot(tables.to[kind][...], df, high)
        grad = grad * spectral_weight(plan.grids[kind], 2 * half)
        gr, gi = grad[:half], grad[half:]
        re, im = spec[off : off + half], spec[off + half : off + 2 * half]
        kr, ki = filter_parts(plan, kind, filt, lk, layer)
        part_r = gr * re + gi * im
        part_i = gi * re - gr * im
        if kind == "g":
            filt_sum = [filt_sum[0] + part_r, filt_sum[1] + part_i]
        else:
            for i in range(plan.group):
                cut = slice(i * LSPEC, (i + 1) * LSPEC)
                local_sum = [local_sum[0] + part_r[cut], local_sum[1] + part_i[cut]]
        back = jnp.concatenate([gr * kr + gi * ki, gi * kr - gr * ki], 0)
        dz = dot(tables.back_to[kind][...], back, high)
        normal = n1[rs]
        sums[0] = sums[0] + jnp.sum(dz * normal, 0, keepdims=True)
        sums[1] = sums[1] + jnp.sum(dz, 0, keepdims=True)
        dx[rs] = dx[rs] + normalize_back(dz, g1, normal, s1[rs])
    for c in range(2):
        filt_sum[c] = filt_sum[c] + lax.dot_general(
            dlk[...],
            local_sum[c],
            (((0,), (0,)), ((), ())),
            preferred_element_type=f32,
            precision=high,
        )
    return sums, filt_sum


def place_blocks(net, me, pieces, shard, cols, both, sem):
    for array, masks in pieces:
        for j, mask in enumerate(masks):
            d, t = net.place(me, mask)
            rows_at = pl.ds(pl.multiple_of(d * shard, 16), shard)
            cols_at = pl.ds(pl.multiple_of(t * cols, 128), cols)
            for i, matrix in enumerate(both):
                start_copy(
                    array.at[j, pl.ds(i * shard, shard)], matrix.at[rows_at, cols_at], sem.at[i]
                )


def cut_blocks(net, me, shard, cols, both, outs, sem):
    unit = len(net.masks(1))
    for i, mask in enumerate(net.masks(0)):
        d, t = net.place(me, mask)
        rows_at = pl.ds(pl.multiple_of(d * shard, 16), shard)
        cols_at = pl.ds(pl.multiple_of(t * cols, 128), cols)
        for k, matrix in enumerate(both):
            start_copy(
                matrix.at[rows_at, cols_at],
                outs[i // unit].at[i % unit, pl.ds(k * shard, shard)],
                sem.at[k],
            )


def cut_adam(net, me, share, adam, outs):
    unit = len(net.masks(1))
    for i, mask in enumerate(net.masks(0)):
        own = pl.ds(pl.multiple_of((me ^ mask) * share, 8), share)
        outs[i // unit][i % unit] = pair(adam[own, :])


def gelu_parts(a):
    bell = jnp.exp(-0.5 * a * a)
    t = pl.reciprocal(1.0 + (0.3275911 * 0.7071067811865476) * jnp.abs(a))
    tail = 0.5 * 1.061405429 * t - 0.5 * 1.453152027
    for coefficient in (1.421413741, -0.284496736, 0.254829592):
        tail = tail * t + 0.5 * coefficient
    tail = tail * t * bell
    phi = jnp.where(a >= 0.0, 1.0 - tail, tail)
    return a * phi, phi + (a * bell) * 0.3989422804014327


def ff_forward(layer, u, up_s, dn_s, bias, h, gp, acc):
    tiles = [slice(j, j + TILE) for j in range(0, FF, TILE)]

    def first(cols):
        return dot(u[...], up_s[:, cols]) + bias[layer : layer + 1, cols]

    ahead = first(tiles[0])
    for j, cols in enumerate(tiles):
        a = ahead
        if j + 1 < len(tiles):
            ahead = first(tiles[j + 1])
        act, slope = gelu_parts(a)
        act = act.astype(bf16)
        h[:, cols] = act
        gp[:, cols] = slope
        term = dot_last(act, dn_s[:, cols])
        acc[...] = term if j == 0 else acc[...] + term


def ff_backward(dm, h, gp, up_s, dn_s, dbias, du, weights):
    tiles = [slice(j, j + TILE) for j in range(0, FF, TILE)]

    def first(cols):
        return dot(dm[...], dn_s[:, cols])

    ahead = first(tiles[0])
    for j, cols in enumerate(tiles):
        grad = ahead
        if j + 1 < len(tiles):
            ahead = first(tiles[j + 1])
        dpre = (grad * gp[:, cols]).astype(bf16)
        weights(cols, dpre)
        dbias[:, cols] = jnp.sum(dpre.astype(f32), 0, keepdims=True)
        term = dot_last(dpre, up_s[:, cols])
        du[...] = term if j == 0 else du[...] + term


def adam_update(weight, grad, first, second):
    first_new = adam_one * first + (1.0 - adam_one) * grad
    second_new = adam_two * second + (1.0 - adam_two) * grad * grad
    first_hat = first_new / (1.0 - adam_one**STEP)
    second_hat = second_new / (1.0 - adam_two**STEP)
    weight_new = weight * (1.0 - adam_rate * adam_decay) - adam_rate * first_hat / (
        jnp.sqrt(second_hat) + adam_floor
    )
    return (first_new, second_new, weight_new)


def flip(v):
    return v.astype(f32).T.astype(bf16)


def per_device(
    global_tokens,
    local_tokens,
    global_cotangent,
    local_cotangent,
    up_weight,
    down_weight,
    filters,
    resize,
    vectors,
    hidden_bias,
    up_momentum,
    down_momentum,
    filter_means,
    filter_squares,
    vector_means,
    vector_squares,
    bias_means,
    bias_squares,
):
    both = ("dp", "tensor")
    net = Net(lax.axis_size("dp"), lax.axis_size("tensor"))
    parts, across, devices = net.parts, net.across, net.devices
    micro, global_images = global_tokens.shape[:2]
    local_images = local_tokens.shape[1]
    layers, shard, cols = up_weight.shape
    direct = net.power and shard % 16 == 0 and cols == D
    plan = Plan(micro, global_images, local_images)
    rows, spec_rows = plan.rows, plan.spec
    to_tables = {k: jnp.asarray(t) for k, t in plan.tables.items()}
    filt = filters.reshape(layers, 2, GSPEC, D)
    down_t = jnp.swapaxes(down_weight, 1, 2)
    down_momentum_t = jnp.swapaxes(down_momentum, 1, 2)
    vec = jnp.swapaxes(vectors, 0, 1)
    vec_at = 2 * GSPEC
    bias_at = vec_at + 5
    adam_used = bias_at + FF // D
    share = round_up((adam_used + devices - 1) // devices, 8)
    adam_rows = devices * share if direct else round_up(adam_used, 8)
    matrix = struct((D, FF), bf16)
    row_f32 = struct((rows, D), f32)
    row_bf16 = struct((rows, D), bf16)
    column = struct((rows, 1), f32)
    flat = struct((D, rows), bf16)
    hidden = struct((rows, FF), bf16)
    hidden_f32 = struct((rows, FF), f32)
    unit = len(net.masks(1))
    inner = net.masks(2)
    inner1 = inner

    def piece_masks(inside):
        unit_at, size = net.stages[1]
        return [[c + i * unit_at + m for m in inside] for c in range(2) for i in range(size)]

    def whole(got):
        got = got.reshape(parts, across, -1, shard, cols)
        return got.transpose(2, 0, 3, 1, 4).reshape(got.shape[2], D, FF)

    def hold(current, token):
        return gate([current], token)[0] if direct else current

    def gather_near(current, later=None):
        if not direct:
            return far(whole(lax.all_gather(current.reshape(1, -1, cols), both, axis=0, tiled=True)))
        pieces = net.gather_plane(current)
        if later is not None:
            pieces = list(gate(pieces, later))
        return far(net.gather_core(pieces))

    def unpack(operand, inside, matrices, sem):
        if direct:
            pieces = list(zip(operand, piece_masks(inside)))
            place_blocks(net, net.me(), pieces, shard, cols, matrices, sem)
        else:
            for i, m in enumerate(matrices):
                start_copy(operand.at[i], m, sem.at[i])

    def arrived(matrices, sem):
        for i, m in enumerate(matrices):
            wait_copy(m, sem.at[i])

    def give(ins, matrices, outs, sem):
        if direct:
            cut_blocks(net, net.me(), shard, cols, matrices, outs, sem)
        else:
            for i, m in enumerate(matrices):
                start_copy(m, outs[i], sem.at[i])

    grad_shapes = [struct((unit, 2 * shard, D), bf16)] * 2 if direct else [matrix] * 2
    saved_shapes = Box(
        n1=row_f32, s1=column, spec=struct((spec_rows, D), f32), n2=row_f32, s2=column, u=row_bf16
    )
    norm_names = ("n1", "s1", "spec", "n2", "s2")
    chunk_shape = struct((1, 2 * shard, cols), bf16)

    def cast_body(ins, outs, s, sems):
        names = ("up", "dn")
        for i, name in enumerate(names):
            start_copy(ins[name], s[name], sems.given.at[i])
        for i, name in enumerate(names):
            wait_copy(s[name], sems.given.at[i])
            for layer, out in enumerate(outs.chunks):
                out[0, i * shard : (i + 1) * shard] = s[name][layer].astype(bf16)

    block_shape = struct((layers, shard, cols), f32)
    low_weights = call(
        cast_body,
        far(Box(up=up_weight, dn=down_t)),
        Box(chunks=[chunk_shape] * layers),
        Box(up=block_shape, dn=block_shape),
        Box(given=2),
        limit=8 * MIB,
    )
    reached = list(low_weights.chunks)
    if direct:
        reached[0] = net.gather_far(reached[0])
        reached[1], inner1 = net.gather_bits(gate([reached[1]], reached[0])[0])

    def pre_body(ins, outs, s, sems):
        for layer in range(layers):
            for c in range(2):
                outs.lk[layer, c] = dot(ins.resize[...], ins.filt[layer, c], high)
        for seg in plan.segments:
            load_rows(plan, seg, outs.x, ins.gt, ins.lt)
            load_rows(plan, seg, outs.dx, ins.gc, ins.lc)
        for kind, table in ins.to.items():
            outs.back_to[kind][...] = table[...].T
        tables = Box(to=ins.to, back_to=outs.back_to)
        pre_layer(plan, 0, outs.x, ins.vec, ins.filt, outs.lk, tables, **outs.saved)

    pre = call(
        pre_body,
        Box(
            gt=global_tokens, lt=local_tokens, gc=global_cotangent, lc=local_cotangent, vec=vec,
            filt=filt, resize=resize, to=to_tables,
        ),
        Box(
            x=row_f32, dx=row_f32, lk=struct((layers, 2, LSPEC, D), f32), saved=saved_shapes,
            back_to={k: struct(t.shape[::-1], f32) for k, t in to_tables.items()},
        ),
        limit=10 * MIB,
    )
    saved0, lk = pre.saved, pre.lk
    tables = Box(to=to_tables, back_to=pre.back_to)
    if direct:
        reached[1] = gate([reached[1]], lk)[0]
    weights0 = gather_near(reached[0], reached[1])
    reached1 = hold(reached[1], weights0[len(weights0) // 2 - 1].array) if direct else reached[1]

    def first_body(ins, outs, s, sems):
        unpack(ins.w, inner, outs.w, sems.w)
        arrived(outs.w, sems.w)
        ff_forward(0, ins.u, *outs.w, ins.bias, outs.h, outs.gp, s.acc)
        outs.x[...] = ins.x[...] + s.acc[...] + ins.vec[4, 0:1]

    first = call(
        first_body,
        Box(
            w=weights0, x=pre.x, u=saved0.u, vec=vec, bias=hidden_bias,
            token=far(reached1),
        ),
        Box(h=hidden, gp=hidden_f32, w=[matrix] * 2, x=row_f32),
        Box(acc=row_f32),
        Box(w=2),
        weight=9,
        limit=16 * MIB,
    )
    weights1 = gather_near(reached1, first.x)

    def middle_body(ins, outs, s, sems):
        pre_layer(plan, 1, ins.x, ins.vec, ins.filt, ins.lk, ins.tables, **outs)

    saved1 = call(
        middle_body,
        Box(x=first.x, vec=vec, filt=filt, lk=lk, tables=tables),
        saved_shapes,
        weight=4,
        limit=10 * MIB,
    )

    backward_scratch = Box(grads=[matrix] * 2, dmt=flat, ut=flat)

    def weight_gradients(s, grad, u, h):
        s.dmt[...] = grad.astype(f32).T.astype(bf16)
        s.ut[...] = flip(u[...])

        def tile(cols, dpre):
            s.grads[1][:, cols] = dot(s.dmt[...], h[:, cols]).astype(bf16)
            s.grads[0][:, cols] = dot(s.ut[...], dpre).astype(bf16)

        return tile

    def norms_back(layer, ins, du, dx, saved, tables_ref, shift, dbias, adam, out):
        sums, filt_sum = pre_layer_back(
            plan, layer, du, dx, ins.vec, ins.filt, ins.lk, tables_ref,
            dlk=ins.resize, **{k: saved[k] for k in norm_names},
        )
        for c in range(2):
            adam[c * GSPEC : (c + 1) * GSPEC] = filt_sum[c]
        for i in range(4):
            adam[vec_at + i : vec_at + i + 1] = sums[i]
        adam[vec_at + 4 : vec_at + 5] = shift[...]
        for i in range(FF // D):
            adam[bias_at + i : bias_at + i + 1] = dbias[:, i * D : (i + 1) * D]
        if adam_rows > adam_used:
            adam[adam_used:] = jnp.zeros((adam_rows - adam_used, D), f32)
        if direct:
            cut_adam(net, net.me(), share, adam, out)
        else:
            out[0][...] = adam[...]

    adam_shape = struct((adam_rows, D), f32)
    adam_shapes = [struct((unit, 2 * share, D), bf16)] * 2 if direct else [adam_shape]
    line = struct((1, D), f32)
    wide_line = struct((1, FF), f32)

    def second_body(ins, outs, s, sems):
        saved = ins.saved
        unpack(ins.w, inner1, s.w, sems.w)
        arrived(s.w, sems.w)
        ff_forward(1, saved.u, *s.w, ins.bias, s.h, s.gp, s.acc)
        outs.y[...] = ins.x[...] + s.acc[...] + ins.vec[4, 1:2]
        grad = ins.dx[...].astype(bf16)
        s.dm[...] = grad
        outs.shift[...] = jnp.sum(grad.astype(f32), 0, keepdims=True)
        tile = weight_gradients(s, grad, saved.u, s.h)
        ff_backward(s.dm, s.h, s.gp, *s.w, outs.dbias, outs.du, tile)
        give(ins, s.grads, outs.grads, sems.taken)
        arrived(s.grads, sems.taken)

    second = call(
        second_body,
        Box(w=weights1, x=first.x, saved=saved1, vec=vec, bias=hidden_bias, dx=pre.dx),
        Box(
            y=row_f32,
            grads=far(grad_shapes),
            du=row_f32,
            dbias=wide_line,
            shift=line,
        ),
        Box(acc=row_f32, h=hidden, gp=hidden_f32, w=[matrix] * 2, dm=row_bf16, **backward_scratch),
        Box(w=2, taken=2),
        weight=14,
        limit=25 * MIB,
    )

    def branch_body(ins, outs, s, sems):
        outs.dx[...] = ins.dx[...]
        norms_back(
            1, ins, ins.du, outs.dx, ins.saved, ins.tables, ins.shift, ins.dbias, s.adam, outs.adam
        )

    branch = call(
        branch_body,
        Box(
            du=second.du, dx=pre.dx, saved=saved1, shift=second.shift, dbias=second.dbias, vec=vec,
            filt=filt, lk=lk, resize=resize, tables=tables,
        ),
        Box(dx=row_f32, adam=adam_shapes),
        Box(adam=adam_shape),
        weight=3,
        limit=12 * MIB,
    )
    if direct:
        terms1 = net.exchange(0, second.grads)
        pairs1 = net.exchange(0, branch.adam)
        terms1 = sum_stage(terms1, pairs1, net.stages[1][1])
    else:
        terms1 = second.grads

    def third_body(ins, outs, s, sems):
        grad = ins.dx[...].astype(bf16)
        s.dm[...] = grad
        outs.shift[...] = jnp.sum(grad.astype(f32), 0, keepdims=True)
        tile = weight_gradients(s, grad, ins.u, ins.h)
        ff_backward(
            s.dm, ins.h, ins.gp, *ins.w, outs.dbias, outs.du, tile
        )
        give(ins, s.grads, outs.grads, sems.taken)
        arrived(s.grads, sems.taken)

    third = call(
        third_body,
        Box(
            w=first.w, dx=branch.dx, u=saved0.u, h=first.h, gp=first.gp, token=far(terms1[0])
        ),
        Box(grads=far(grad_shapes), du=row_f32, dbias=wide_line, shift=line),
        Box(dm=row_bf16, **backward_scratch),
        Box(taken=2),
        limit=12 * MIB,
    )
    grads0 = third.grads
    def fourth_body(ins, outs, s, sems):
        s.dx[...] = ins.dx[...]
        norms_back(
            0, ins, ins.du, s.dx, ins.saved, ins.tables, ins.shift,
            ins.dbias, s.adam, outs.adam,
        )
        for seg in plan.segments:
            store_rows(plan, seg, s.dx, outs.ggrad, outs.lgrad, False)
            store_rows(plan, seg, ins.y, outs.gout, outs.lout, True)

    fourth = call(
        fourth_body,
        Box(
            y=second.y,
            dx=branch.dx, du=third.du, dbias=third.dbias, shift=third.shift,
            saved={k: saved0[k] for k in norm_names}, vec=vec, filt=filt, lk=lk,
            resize=resize, tables=tables, token=far(terms1[0]),
        ),
        Box(
            gout=struct((global_images, TOKG, micro, D), bf16),
            lout=struct((micro, TOKL, local_images, D), bf16),
            ggrad=struct((micro, TOKG, global_images, D), f32),
            lgrad=struct((micro, TOKL, local_images, D), f32),
            adam=adam_shapes,
        ),
        Box(dx=row_f32, adam=adam_shape),
        limit=10 * MIB,
    )

    block = struct((shard, cols), f32)

    def momentum(layer, terms, token=(), others=None):
        if not direct:
            terms = jnp.stack(terms).reshape(2, parts, shard, across, cols)
            terms = terms.transpose(1, 3, 0, 2, 4).reshape(devices * 2, shard, cols)
            mine = lax.psum_scatter(terms, both, scatter_dimension=0, tiled=True).astype(f32)
            up = momentum_decay * up_momentum[layer] + mine[0]
            dn = momentum_decay * down_momentum_t[layer] + mine[1]
            return Box(up=up, dn=dn, chunk=jnp.concatenate([up, dn], 0).astype(bf16)[None])
        chunk = terms[0].shape[1]

        def body(ins, outs, s, sems):
            for i, name in enumerate(("up", "dn")):
                at = slice(i * shard, (i + 1) * shard)
                velocity = momentum_decay * ins[name][layer] + add_terms(ins.terms, (0, at))
                if others is None:
                    outs[name][...] = velocity
                else:
                    outs[name][layer] = velocity
                    outs[name][1 - layer] = ins.others[i][...]
                outs.chunk[0, at] = velocity.astype(bf16)
            outs.chunk[0, 2 * shard :] = pair(
                add_pairs(ins.terms, (0, slice(2 * shard, chunk)))
            )

        shape = block if others is None else block_shape
        return call(
            body,
            Box(
                terms=terms, up=up_momentum, dn=down_momentum_t, token=far(token),
                others=() if others is None else others,
            ),
            Box(up=shape, dn=shape, chunk=struct((1, chunk, D), bf16)),
            weight=0 if others is None else 20,
            limit=8 * MIB,
        )

    shown = [jnp.transpose(fourth.gout, (2, 0, 1, 3))] + [
        jnp.swapaxes(a, 1, 2) for a in (fourth.lout, fourth.ggrad, fourth.lgrad)
    ]
    if direct:
        cuts = [size for _, size in net.stages] + [1]
        terms1 = sum_stage(net.exchange(1, terms1), (), cuts[2], 2 * share, (), 20)
        terms0, pairs0 = net.exchange(0, grads0), net.exchange(0, fourth.adam)
        terms0 = sum_stage(terms0, pairs0, cuts[1], token=terms1[0])
        next0 = net.exchange(1, terms0)
        if len(net.stages) == 3:
            new1 = momentum(1, net.exchange(2, terms1), terms0[0])
            terms0 = sum_stage(next0, (), cuts[2], 2 * share, new1.chunk)
        else:
            terms0 = sum_stage(next0, (), cuts[2], 2 * share)
        for index in range(2, len(net.stages)):
            if index + 1 < len(net.stages):
                terms1 = net.exchange(index, terms1)
                terms1 = sum_stage(terms1, (), cuts[index + 1], 2 * share, terms0[0])
                terms0 = net.exchange(index, terms0)
                terms0 = sum_stage(terms0, (), cuts[index + 1], 2 * share, terms1[0])
        if len(net.stages) > 3:
            new1 = momentum(1, net.exchange(len(net.stages) - 1, terms1), terms0[0])
        new0 = momentum(
            0, net.exchange(len(net.stages) - 1, terms0), (), (new1.up, new1.dn)
        )
        reached1, inner1 = net.gather_bits(new1.chunk, (terms0[0], new0.chunk))
        up_velocity, down_velocity = new0.up, new0.dn
    else:
        new1 = momentum(1, terms1)
        new0 = momentum(0, grads0)
        up_velocity, down_velocity = (jnp.stack([new0[k], new1[k]]) for k in ("up", "dn"))

    scale_out = muon_rate * 0.2 * math.sqrt(max(D, FF))

    def eye():
        return (
            lax.broadcasted_iota(jnp.int32, (D, D), 0) == lax.broadcasted_iota(jnp.int32, (D, D), 1)
        ).astype(f32)

    def polynomial(gram, gram_s, poly_s, rows_at):
        one = eye()
        scale = 1.0 / (jnp.sqrt(jnp.sum(gram * one, keepdims=True)) + 1e-07)
        gram = gram * (scale * scale)
        gram_s[...] = gram
        poly_s[...] = ns_a * one + ns_b * gram + ns_c * dot(gram, gram, high)
        chain = [poly_s[rows_at]]
        for _ in range(2):
            row = chain[-1]
            for factor in (poly_s, gram_s, poly_s):
                row = dot(row, factor[...], high)
            chain.append(row)
        return (ns_a * chain[0] + ns_b * chain[1] + ns_c * chain[2]) * scale

    square = struct((D, D), f32)
    old = Box(up=up_weight, dn=down_t)
    names = ("up", "dn")

    def new_weight(old_weight, q_rows, v):
        orth = dot(q_rows, v)
        return old_weight * (1.0 - muon_rate * muon_decay) - scale_out * orth

    adam_ins = Box(
        filt=(filt, filter_means.reshape(filt.shape), filter_squares.reshape(filt.shape)),
        vec=(vec, jnp.swapaxes(vector_means, 0, 1), jnp.swapaxes(vector_squares, 0, 1)),
        bias=(hidden_bias, bias_means, bias_squares),
    )
    adam_shapes_out = jax.tree.map(lambda a: struct(a.shape, f32), adam_ins)
    adam_count = len(jax.tree.leaves(adam_ins))

    def adam_step(ins, outs, name, at, grad):
        old, mean, square = (ref[at] for ref in ins[name])
        for ref, value in zip(outs[name], adam_update(old, grad, mean, square)):
            ref[at] = value

    def adam_lines(ins, outs, layer, rows_at):
        for i in range(5):
            adam_step(ins, outs, "vec", (i, slice(layer, layer + 1)), rows_at(i))
        for i in range(FF // D):
            at = (slice(layer, layer + 1), slice(i * D, (i + 1) * D))
            adam_step(ins, outs, "bias", at, rows_at(5 + i))

    def copies(pairs, sems, action):
        for i, (src, dst) in enumerate(pairs):
            getattr(pltpu.make_async_copy(src, dst, sems.at[i]), action)()

    def muon_whole():
        moved = [
            whole(lax.all_gather(new.chunk[0].reshape(1, -1, cols), both, axis=0, tiled=True))
            for new in (new0, new1)
        ]
        start = lax.axis_index("dp") * shard

        def widen(weight):
            wide = jnp.zeros((layers, D, cols), f32)
            return lax.dynamic_update_slice_in_dim(wide, weight, start, 1)

        def body(ins, outs, s, sems):
            for layer in range(layers):
                total = ins.total.at[layer]
                for c in range(2):
                    rows_in = total[c * GSPEC : (c + 1) * GSPEC]
                    adam_step(ins.adam, outs.adam, "filt", (layer, c), rows_in)
                adam_lines(
                    ins.adam, outs.adam, layer, lambda i: total[vec_at + i : vec_at + i + 1]
                )
            cols_at = pl.ds(pl.multiple_of((net.me() % across) * cols, 128), cols)
            for layer in range(layers):
                for i, name in enumerate(names):
                    v = ins.v[layer][i]
                    q = polynomial(dot_last(v, v), s.gram, s.poly, slice(0, D))
                    part = ins.v[layer][i, :, cols_at]
                    outs[name][layer] = new_weight(ins.old[name][layer], q.astype(bf16), part)

        wide = struct((layers, D, cols), f32)
        last = call(
            body,
            Box(
                v=moved, old={k: widen(v) for k, v in old.items()}, adam=adam_ins,
                total=lax.psum(jnp.stack([fourth.adam[0], branch.adam[0]]), both),
            ),
            Box(up=wide, dn=wide, adam=adam_shapes_out),
            Box(gram=square, poly=square),
            limit=48 * MIB,
        )
        up, dn = (lax.dynamic_slice_in_dim(last[k], start, shard, 1) for k in names)
        return up, dn, last.adam

    def muon_direct():
        core_unit, far_unit = 1, 2
        half = D // 3
        places = [(0, 0), (0, 1), (0, 2), (1, 1), (1, 2), (2, 2)]
        tall = 2 * half
        far_bits = [2**b for b in range(2, net.bits) if 2**b < net.stages[1][0] * net.stages[1][1]]
        column_masks = []
        for masks in (inner, inner1):
            for bit in far_bits:
                masks = masks + [bit + m for m in masks]
            column_masks.append(masks)
        mine_rows = len(column_masks[0]) * share

        def pack(gram, out, start):
            for k, (r, c) in enumerate(places):
                at = pl.ds(start + (k // 3) * half, half)
                block_of = gram[r * half : (r + 1) * half, c * half : (c + 1) * half]
                out[at, (k % 3) * half : (k % 3 + 1) * half] = block_of.astype(bf16)

        def unpack_gram(terms, out):
            for k, (r, c) in enumerate(places):
                at = (pl.ds((k // 3) * half, half), pl.ds((k % 3) * half, half))
                value = terms[0][at].astype(f32) + terms[1][at].astype(f32)
                out[r * half : (r + 1) * half, c * half : (c + 1) * half] = value
                if r != c:
                    out[c * half : (c + 1) * half, r * half : (r + 1) * half] = value.T

        def gram_stage(layer, pieces, token):
            def body(ins, outs, s, sems):
                me_at = net.me()
                index = 0
                for array in ins.pieces:
                    for j in range(array.shape[0]):
                        d, _ = net.place(me_at, column_masks[layer][index])
                        at = pl.ds(pl.multiple_of(d * shard, 16), shard)
                        for i in range(2):
                            outs.v[i, at] = array[j, i * shard : (i + 1) * shard]
                        sums = add_pairs([array], (j, slice(2 * shard, 2 * shard + 2 * share)))
                        s.adam[index * share : (index + 1) * share] = sums
                        index += 1
                for i in range(2):
                    v = outs.v[i]
                    s.gram[i] = dot_last(v, v)
                core = me_at & 1
                pack(s.gram.at[core], outs.keep, 0)
                pack(s.gram.at[1 - core], outs.send, 0)
                rows_out = s.adam[...].astype(bf16)
                outs.send[tall:] = rows_out
                outs.adam[...] = rows_out

            return call(
                body,
                Box(pieces=pieces, token=far(token)),
                Box(
                    v=struct((2, D, cols), bf16),
                    keep=struct((tall, D), bf16),
                    adam=struct((mine_rows, D), bf16),
                    send=struct((tall + mine_rows, D), bf16),
                ),
                Box(gram=struct((2, D, D), f32), adam=struct((mine_rows, D), f32)),
                limit=16 * MIB,
            )

        def core_sum(keep, got, token):
            def body(ins, outs, s, sems):
                keep_ref, got_ref = ins.keep, ins.got
                outs[...] = (keep_ref[...].astype(f32) + got_ref[:tall].astype(f32)).astype(bf16)

            return call(
                body,
                Box(keep=keep, got=got, token=far(token)),
                struct((tall, D), bf16),
                limit=4 * MIB,
            )

        def pick_stage(keep, got, other):
            def body(ins, outs, s, sems):
                keep_ref, got_ref = ins.keep, ins.got
                x = (net.me() >> 1) & 1
                s.both[0] = (
                    keep_ref[...].astype(f32) + got_ref[:tall].astype(f32)
                ).astype(bf16)
                s.both[1] = ins.other[...]
                outs.mine[...] = s.both[x]
                outs.send[...] = s.both[1 - x]

            return call(
                body,
                Box(keep=keep, got=got, other=other),
                Box(mine=struct((tall, D), bf16), send=struct((tall, D), bf16)),
                Box(both=struct((2, tall, D), bf16)),
                limit=4 * MIB,
            )

        def poly_stage(mine, got):
            def body(ins, outs, s, sems):
                unpack_gram((ins.mine, ins.got), s.sum)
                d, _ = net.place(net.me(), 0)
                rows_at = pl.ds(pl.multiple_of(d * shard, 8), shard)
                q = polynomial(s.sum[...], s.gram, s.poly, rows_at)
                outs[...] = q.astype(bf16)

            return call(
                body,
                Box(mine=mine, got=got),
                struct((shard, D), bf16),
                Box(sum=square, gram=square, poly=square),
                weight=3,
                limit=8 * MIB,
            )

        def final_stage(vs, qs):
            def body(ins, outs, s, sems):
                at = net.me() & 3
                for mask, q in enumerate(ins.qs):
                    s.q[at ^ mask] = q[...]
                for layer in range(layers):
                    for i, name in enumerate(names):
                        q_rows = s.q[2 * layer + i]
                        outs[name][layer] = new_weight(
                            ins.old[name][layer], q_rows, ins.vs[layer][i]
                        )

            return call(
                body,
                Box(vs=vs, qs=qs, old=old),
                Box(up=block_shape, dn=block_shape),
                Box(q=struct((4, shard, D), bf16)),
                limit=6 * MIB,
            )

        line_rows = adam_rows - vec_at

        def mark_of(tree, key):
            marks = Box({k: jax.tree.map(lambda _: k == key, v) for k, v in tree.items()})
            return [i for i, mark in enumerate(jax.tree.leaves(marks)) if mark]

        def adam_stage(layer, columns, before, token=()):
            last = before is not None
            kinds = ("vec", "bias") if last else ()

            def body(ins, outs, s, sems):
                filts = [ref.at[layer] for ref in ins.adam.filt]
                filts_out = [ref.at[layer] for ref in outs.filt]
                whole_in = [(r, t) for k in kinds for r, t in zip(ins.adam[k], s.given[k])]
                loads = list(zip(filts, s.given.filt)) + whole_in
                copies(loads, sems.given, "start")
                for number, array in enumerate(ins.columns):
                    first_row = columns[number][1]
                    values = array[first_row : first_row + mine_rows].astype(f32)
                    for i, mask in enumerate(column_masks[layer]):
                        at = (net.me() ^ (mask | number)) * share
                        s.total[pl.ds(pl.multiple_of(at, 8), share)] = values[
                            i * share : (i + 1) * share
                        ]
                copies(loads, sems.given, "wait")
                for c in range(2):
                    grad = s.total[c * GSPEC : (c + 1) * GSPEC]
                    adam_step(s.given, s.taken, "filt", c, grad)
                stores = list(zip(s.taken.filt, filts_out))
                if last:
                    for number, ref, start in ((layer, s.total, vec_at), (1 - layer, ins.lines, 0)):
                        adam_lines(
                            s.given, s.taken, number,
                            lambda i, ref=ref, start=start: ref[start + i : start + i + 1],
                        )
                    stores += [(t, r) for k in kinds for t, r in zip(s.taken[k], outs[k])]
                else:
                    outs.lines[...] = s.total[vec_at:]
                copies(stores, sems.taken, "start")
                copies(stores, sems.taken, "wait")

            part = Box(filt=[struct(filt.shape[1:], f32)] * 3, **{k: adam_shapes_out[k] for k in kinds})
            ins = Box(adam=far(adam_ins), columns=[a for a, _ in columns], token=far(token))
            outs = Box(filt=far(list(adam_shapes_out.filt)))
            aliases = None
            if last:
                outs.update({k: far(adam_shapes_out[k]) for k in kinds})
                ins.lines = before.lines
                ins.done = far(before.filt)
                marks = mark_of(ins, "done")
                aliases = dict(zip(marks, mark_of(outs, "filt")))
            else:
                outs.lines = struct((line_rows, D), f32)
            count = 3 + 3 * len(kinds)
            return call(
                body,
                ins,
                outs,
                Box(given=part, taken=part, total=struct((adam_rows, D), f32)),
                Box(given=count, taken=count),
                weight=2,
                limit=8 * MIB,
                aliases=aliases,
            )

        def column(array):
            pieces = [array]
            for bit in far_bits:
                pieces = pieces + [net.swap(p, bit) for p in pieces]
            return pieces

        reached0 = net.gather_far(new0.chunk)
        gram1 = gram_stage(1, column(reached1), reached0)
        far1 = [net.swap(gram1.adam, mask) for mask in (2, 3)]
        gram0 = gram_stage(0, column(reached0), far1)
        got1, got0 = (net.swap(gram.send, core_unit) for gram in (gram1, gram0))
        rows1 = [(gram1.adam, 0), (got1, tall)] + [(a, 0) for a in far1]
        sum1 = core_sum(gram1.keep, got1, gram0.keep)
        picked = pick_stage(gram0.keep, got0, sum1)
        adam1 = adam_stage(1, rows1, None, picked.mine)
        q = poly_stage(picked.mine, net.swap(picked.send, far_unit))
        (late,) = gate([gram0.adam], adam1.lines)
        rows0 = [(late, 0), (got0, tall)] + [(net.swap(late, mask), 0) for mask in (2, 3)]
        adam_outs = adam_stage(0, rows0, adam1)
        qs = [q] + [net.swap(q, mask) for mask in (1, 2, 3)]
        final = final_stage([gram0.v, gram1.v], qs)
        return final.up, final.dn, adam_outs

    if direct:
        up_master, down_master, adam_outs = muon_direct()
    else:
        up_master, down_master, adam_outs = muon_whole()
    filter_mean, filter_square, filter_master = (
        a.reshape(filters.shape) for a in adam_outs.filt
    )
    vector_mean, vector_square, vector_master = (
        jnp.swapaxes(a, 0, 1) for a in adam_outs.vec
    )
    bias_mean, bias_square, bias_master = adam_outs.bias
    return (
        *shown,
        up_velocity,
        up_master,
        jnp.swapaxes(down_velocity, 1, 2),
        jnp.swapaxes(down_master, 1, 2),
        filter_mean,
        filter_square,
        filter_master,
        vector_mean,
        vector_square,
        vector_master,
        bias_mean,
        bias_square,
        bias_master,
    )


def solution(mesh):
    images = P(None, ("dp", "tensor"), None, None)
    up, down = P(None, "dp", "tensor"), P(None, "tensor", "dp")
    in_specs = (images,) * 4 + (up, down) + (P(),) * 4 + (up, down) + (P(),) * 6
    out_specs = (images,) * 4 + (up, up, down, down) + (P(),) * 9
    return jax.shard_map(
        per_device, mesh=mesh, in_specs=in_specs, out_specs=out_specs, check_vma=False
    )
```

```python
import math

import jax
import jax.numpy as jnp
import numpy as np
from jax import lax
from jax.experimental import pallas as pl
from jax.experimental.pallas import tpu as pltpu
from jax.sharding import PartitionSpec as P

D = 384
FF = 1536
GRID = 14
LGRID = 6
TOKG = GRID * GRID
TOKL = LGRID * LGRID
GSPEC = 112
LSPEC = 24
STEP = 5
TILE = 256
SCALE = 1.15e9
MIB = 1024 * 1024

high = lax.Precision.HIGH
epsilon_norm = 1e-06
ns_a = 3.4445
ns_b = -4.775
ns_c = 2.0315
momentum_decay = 0.95
muon_rate = 0.25
muon_decay = 0.01
adam_one = 0.9
adam_two = 0.95
adam_rate = 0.25
adam_decay = 0.01
adam_floor = 1e-08
contract_last = (((1,), (1,)), ((), ()))
f32 = jnp.float32
bf16 = jnp.bfloat16


def round_up(value, unit):
    return (value + unit - 1) // unit * unit


def dft_table(grid, copies, rows):
    freq_count = grid // 2 + 1
    spec = np.arange(grid * freq_count)
    cell = np.arange(grid * grid)
    phase = (
        np.outer(spec // freq_count, cell // grid) + np.outer(spec % freq_count, cell % grid)
    ) % grid
    theta = 2.0 * np.pi / grid * phase
    eye = np.eye(copies)
    table = np.concatenate([np.kron(eye, np.cos(theta)), np.kron(eye, -np.sin(theta))], 0)
    return np.pad(table, ((0, 0), (0, rows - table.shape[1]))).astype(np.float32)


def spectral_weight(grid, rows):
    freq_count = grid // 2 + 1
    second = lax.rem(lax.broadcasted_iota(jnp.int32, (rows, D), 0), jnp.int32(freq_count))
    once = (second == 0) | (2 * second == grid)
    return jnp.where(once, 1.0, 2.0).astype(f32) / (grid * grid)


class Plan:
    def __init__(self, micro, global_images, local_images):
        self.micro = micro
        self.group = 4 if local_images % 4 == 0 else local_images
        self.g_rows = round_up(TOKG, 16)
        self.l_rows = round_up(self.group * TOKL, 16)
        self.segments = []
        row = spec = 0
        for m in range(micro):
            for image in range(global_images):
                self.segments.append(("g", m, image, row, self.g_rows, spec, GSPEC))
                row += self.g_rows
                spec += 2 * GSPEC
            for image in range(0, local_images, self.group):
                half = self.group * LSPEC
                self.segments.append(("l", m, image, row, self.l_rows, spec, half))
                row += self.l_rows
                spec += 2 * half
        self.rows = row
        self.spec = spec
        self.tables = {
            "g": dft_table(GRID, 1, self.g_rows), "l": dft_table(LGRID, self.group, self.l_rows)
        }
        self.grids = {"g": GRID, "l": LGRID}


def dot(a, b, precision=None):
    return jnp.dot(a, b, preferred_element_type=f32, precision=precision)


def dot_last(a, b):
    return lax.dot_general(a, b, contract_last, preferred_element_type=f32)


def load_rows(plan, seg, dst, g_ref, l_ref):
    kind, m, image, row, rows, _, _ = seg
    if kind == "g":
        if rows != TOKG:
            start = TOKG // 8 * 8
            dst[row + start : row + rows] = jnp.zeros((rows - start, D), f32)
        dst[row : row + TOKG] = g_ref[m, image].astype(f32)
    else:
        used = plan.group * TOKL
        if rows != used:
            start = used // 8 * 8
            dst[row + start : row + rows] = jnp.zeros((rows - start, D), f32)
        for i in range(plan.group):
            dst[row + i * TOKL : row + (i + 1) * TOKL] = l_ref[m, image + i].astype(f32)


def store_rows(plan, seg, src, g_ref, l_ref, micro_inner):
    kind, m, image, row, _, _, _ = seg
    if kind == "g":
        value = src[row : row + TOKG].astype(g_ref.dtype)
        if micro_inner:
            g_ref[image, :, m, :] = value
        else:
            g_ref[m, :, image, :] = value
    else:
        for i in range(plan.group):
            value = src[row + i * TOKL : row + (i + 1) * TOKL].astype(l_ref.dtype)
            l_ref[m, :, image + i, :] = value


def normalize(v):
    center = v - jnp.mean(v, -1, keepdims=True)
    scale = lax.rsqrt(jnp.mean(center * center, -1, keepdims=True) + epsilon_norm)
    return center * scale, scale


def normalize_back(dout, gain, normal, scale):
    dn = dout * gain
    return scale * (
        dn
        - jnp.mean(dn, -1, keepdims=True)
        - normal * jnp.mean(dn * normal, -1, keepdims=True)
    )


@jax.tree_util.register_pytree_node_class
class Box(dict):
    __getattr__ = dict.__getitem__
    __setattr__ = dict.__setitem__

    def tree_flatten(self):
        keys = tuple(sorted(self))
        return [self[k] for k in keys], keys

    @classmethod
    def tree_unflatten(cls, keys, values):
        return cls(zip(keys, values))


def struct(shape, dtype):
    return jax.ShapeDtypeStruct(shape, dtype)


class Far:
    def __init__(self, array):
        self.array = array


def far(tree):
    return jax.tree.map(Far, tree)


def call(body, ins, outs, scratch=None, sems=None, weight=0, limit=32 * MIB, aliases=None):
    scratch = {} if scratch is None else scratch
    sems = {} if sems is None else sems
    in_leaves, in_tree = jax.tree.flatten(ins)
    out_leaves, out_tree = jax.tree.flatten(outs)
    scratch_leaves, scratch_tree = jax.tree.flatten(scratch)
    sem_leaves, sem_tree = jax.tree.flatten(sems)

    def kernel(*refs):
        cuts = np.cumsum([len(in_leaves), len(out_leaves), len(scratch_leaves)])
        parts = [refs[: cuts[0]], refs[cuts[0] : cuts[1]], refs[cuts[1] : cuts[2]], refs[cuts[2] :]]
        trees = [in_tree, out_tree, scratch_tree, sem_tree]
        body(*(jax.tree.unflatten(t, p) for t, p in zip(trees, parts)))

    def spec(leaf):
        if isinstance(leaf, Far):
            return pl.BlockSpec(memory_space=pl.ANY)
        return pl.BlockSpec(memory_space=pltpu.SMEM if leaf.dtype == jnp.int32 else pltpu.VMEM)

    def plain(leaf):
        return leaf.array if isinstance(leaf, Far) else leaf

    total = sum(
        math.prod(plain(a).shape) * plain(a).dtype.itemsize for a in in_leaves + out_leaves
    )
    result = pl.pallas_call(
        kernel,
        out_shape=[plain(a) for a in out_leaves],
        in_specs=[spec(a) for a in in_leaves],
        out_specs=[spec(a) for a in out_leaves],
        scratch_shapes=[pltpu.VMEM(a.shape, a.dtype) for a in scratch_leaves]
        + [pltpu.SemaphoreType.DMA((n,)) for n in sem_leaves],
        input_output_aliases={} if aliases is None else aliases,
        compiler_params=pltpu.CompilerParams(vmem_limit_bytes=limit),
        cost_estimate=pl.CostEstimate(
            flops=int(weight * SCALE), bytes_accessed=total if weight else 0, transcendentals=0
        ),
    )(*(plain(a) for a in in_leaves))
    return jax.tree.unflatten(out_tree, result)


def gate(arrays, token):
    count = len(arrays)
    return pl.pallas_call(
        lambda *refs: None,
        out_shape=[struct(a.shape, a.dtype) for a in arrays],
        in_specs=[pl.BlockSpec(memory_space=pl.ANY)] * (count + 1),
        out_specs=[pl.BlockSpec(memory_space=pl.ANY)] * count,
        input_output_aliases={i: i for i in range(count)},
        compiler_params=pltpu.CompilerParams(vmem_limit_bytes=MIB),
    )(*arrays, token)


def start_copy(src, dst, sem):
    pltpu.make_async_copy(src, dst, sem).start()


def wait_copy(like, sem):
    pltpu.make_async_copy(like, like, sem).wait()


def join(arrays, token=()):
    each, rows, _ = arrays[0].shape

    def body(ins, outs, s, sems):
        for i, array in enumerate(ins.arrays):
            for j in range(each):
                outs[i * each + j] = array[j]

    shape = struct((each * len(arrays), rows, D), bf16)
    return call(body, Box(arrays=arrays, token=far(token)), shape, limit=8 * MIB)


class Net:
    def __init__(self, parts, across):
        self.parts, self.across = parts, across
        self.devices = parts * across
        self.bits = self.devices.bit_length() - 1
        self.power = 2**self.bits == self.devices
        self.stages = [(1, 2)]
        bit = 1
        while bit < self.bits:
            width = min(2, self.bits - bit)
            self.stages.append((2**bit, 2**width))
            bit += width

    def me(self):
        return lax.axis_index("dp") * self.across + lax.axis_index("tensor")

    def swap(self, array, mask):
        pairs = [(i, i ^ mask) for i in range(self.devices)]
        return lax.ppermute(array, ("dp", "tensor"), pairs)

    def masks(self, first):
        found = [0]
        for unit, size in reversed(self.stages[first:]):
            found = [i * unit + m for i in range(size) for m in found]
        return found

    def place(self, me, mask):
        other = me ^ mask
        return other >> (self.across.bit_length() - 1), other & (self.across - 1)

    def stack(self, array, index, token=()):
        unit, size = self.stages[index]
        return join([array] + [self.swap(array, i * unit) for i in range(1, size)], token)

    def gather_far(self, chunk, token=()):
        for index in reversed(range(2, len(self.stages))):
            chunk = self.stack(chunk, index, token)
        return chunk

    def gather_bits(self, chunk, tokens=((), ())):
        masks = [0]
        first = self.stages[1][0] * self.stages[1][1]
        bits = [b for b in range(self.bits) if 2**b >= first]
        for bit in reversed(bits):
            token = tokens[1] if bit == bits[0] else tokens[0] if bit == bits[-1] else ()
            chunk = join([chunk, self.swap(chunk, 2**bit)], token)
            masks = masks + [2**bit + m for m in masks]
        return chunk, masks

    def gather_plane(self, current):
        unit, size = self.stages[1]
        return [current] + [self.swap(current, i * unit) for i in range(1, size)]

    def gather_core(self, pieces):
        return pieces + [self.swap(array, 1) for array in pieces]

    def exchange(self, index, arrays):
        unit, size = self.stages[index]
        return [arrays[0]] + [self.swap(arrays[i], i * unit) for i in range(1, size)]


def add_terms(terms, at):
    total = terms[0][at].astype(f32)
    for term in terms[1:]:
        total = total + term[at].astype(f32)
    return total


def pair(total):
    first = total.astype(bf16).astype(f32)
    return jnp.concatenate([first, total - first], 0).astype(bf16)


def add_pairs(terms, at):
    total = add_terms(terms, at)
    half = total.shape[0] // 2
    return total[:half] + total[half:]


def sum_stage(terms, pairs, cuts, pairs_in=0, token=(), weight=0):
    count, rows, _ = terms[0].shape
    rows -= pairs_in
    each = count // cuts
    extra = pairs[0].shape[1] if pairs else pairs_in

    def body(ins, outs, s, sems):
        for i in range(cuts):
            for j in range(each):
                at = i * each + j
                outs[i][j, :rows] = add_terms(ins.terms, (at, slice(0, rows))).astype(bf16)
                if extra:
                    last = slice(0, extra) if pairs else slice(rows, rows + extra)
                    total = add_pairs(ins.pairs if pairs else ins.terms, (at, last))
                    outs[i][j, rows:] = pair(total)

    return call(
        body,
        Box(terms=list(terms), pairs=list(pairs), token=far(token)),
        [struct((each, rows + extra, D), bf16)] * cuts,
        weight=weight,
        limit=6 * MIB,
    )


def filter_parts(plan, kind, filt, lk, layer):
    if kind == "g":
        return filt[layer, 0], filt[layer, 1]
    return (
        jnp.concatenate([lk[layer, 0]] * plan.group, 0),
        jnp.concatenate([lk[layer, 1]] * plan.group, 0),
    )


def pre_layer(plan, layer, x, vec, filt, lk, tables, n1, s1, spec, n2, s2, u):
    g1, b1, g2, b2 = (vec[i, layer : layer + 1] for i in range(4))
    for seg in plan.segments:
        kind, _, _, row, rows, off, half = seg
        rs = slice(row, row + rows)
        normal, scale = normalize(x[rs])
        n1[rs] = normal
        s1[rs] = scale
        z = normal * g1 + b1
        field = dot(tables.to[kind][...], z, high)
        spec[off : off + 2 * half] = field
        kr, ki = filter_parts(plan, kind, filt, lk, layer)
        re, im = field[:half], field[half:]
        out = jnp.concatenate([re * kr - im * ki, re * ki + im * kr], 0)
        out = out * spectral_weight(plan.grids[kind], 2 * half)
        f = dot(tables.back_to[kind][...], out, high)
        normal, scale = normalize(f)
        n2[rs] = normal
        s2[rs] = scale
        u[rs] = (normal * g2 + b2).astype(bf16)


def pre_layer_back(plan, layer, du, dx, vec, filt, lk, tables, n1, s1, spec, n2, s2, dlk):
    g1, g2 = vec[0, layer : layer + 1], vec[2, layer : layer + 1]
    sums = [jnp.zeros((1, D), f32) for _ in range(4)]
    filt_sum = [jnp.zeros((GSPEC, D), f32) for _ in range(2)]
    local_sum = [jnp.zeros((LSPEC, D), f32) for _ in range(2)]
    for seg in plan.segments:
        kind, _, _, row, rows, off, half = seg
        rs = slice(row, row + rows)
        dout, normal = du[rs], n2[rs]
        sums[2] = sums[2] + jnp.sum(dout * normal, 0, keepdims=True)
        sums[3] = sums[3] + jnp.sum(dout, 0, keepdims=True)
        df = normalize_back(dout, g2, normal, s2[rs])
        grad = dot(tables.to[kind][...], df, high)
        grad = grad * spectral_weight(plan.grids[kind], 2 * half)
        gr, gi = grad[:half], grad[half:]
        re, im = spec[off : off + half], spec[off + half : off + 2 * half]
        kr, ki = filter_parts(plan, kind, filt, lk, layer)
        part_r = gr * re + gi * im
        part_i = gi * re - gr * im
        if kind == "g":
            filt_sum = [filt_sum[0] + part_r, filt_sum[1] + part_i]
        else:
            for i in range(plan.group):
                cut = slice(i * LSPEC, (i + 1) * LSPEC)
                local_sum = [local_sum[0] + part_r[cut], local_sum[1] + part_i[cut]]
        back = jnp.concatenate([gr * kr + gi * ki, gi * kr - gr * ki], 0)
        dz = dot(tables.back_to[kind][...], back, high)
        normal = n1[rs]
        sums[0] = sums[0] + jnp.sum(dz * normal, 0, keepdims=True)
        sums[1] = sums[1] + jnp.sum(dz, 0, keepdims=True)
        dx[rs] = dx[rs] + normalize_back(dz, g1, normal, s1[rs])
    for c in range(2):
        filt_sum[c] = filt_sum[c] + lax.dot_general(
            dlk[...],
            local_sum[c],
            (((0,), (0,)), ((), ())),
            preferred_element_type=f32,
            precision=high,
        )
    return sums, filt_sum


def place_blocks(net, me, pieces, shard, cols, both, sem):
    for array, masks in pieces:
        for j, mask in enumerate(masks):
            d, t = net.place(me, mask)
            rows_at = pl.ds(pl.multiple_of(d * shard, 16), shard)
            cols_at = pl.ds(pl.multiple_of(t * cols, 128), cols)
            for i, matrix in enumerate(both):
                start_copy(
                    array.at[j, pl.ds(i * shard, shard)], matrix.at[rows_at, cols_at], sem.at[i]
                )


def cut_blocks(net, me, shard, cols, both, outs, sem):
    unit = len(net.masks(1))
    for i, mask in enumerate(net.masks(0)):
        d, t = net.place(me, mask)
        rows_at = pl.ds(pl.multiple_of(d * shard, 16), shard)
        cols_at = pl.ds(pl.multiple_of(t * cols, 128), cols)
        for k, matrix in enumerate(both):
            start_copy(
                matrix.at[rows_at, cols_at],
                outs[i // unit].at[i % unit, pl.ds(k * shard, shard)],
                sem.at[k],
            )


def cut_adam(net, me, share, adam, outs):
    unit = len(net.masks(1))
    for i, mask in enumerate(net.masks(0)):
        own = pl.ds(pl.multiple_of((me ^ mask) * share, 8), share)
        outs[i // unit][i % unit] = pair(adam[own, :])


def gelu_parts(a):
    bell = jnp.exp(-0.5 * a * a)
    t = pl.reciprocal(1.0 + (0.3275911 * 0.7071067811865476) * jnp.abs(a))
    tail = 0.5 * 1.061405429 * t - 0.5 * 1.453152027
    for coefficient in (1.421413741, -0.284496736, 0.254829592):
        tail = tail * t + 0.5 * coefficient
    tail = tail * t * bell
    phi = jnp.where(a >= 0.0, 1.0 - tail, tail)
    return a * phi, phi + (a * bell) * 0.3989422804014327


def ff_forward(layer, u, up_s, dn_s, bias, h, gp, acc):
    tiles = [slice(j, j + TILE) for j in range(0, FF, TILE)]

    def first(cols):
        return dot(u[...], up_s[:, cols]) + bias[layer : layer + 1, cols]

    ahead = first(tiles[0])
    for j, cols in enumerate(tiles):
        a = ahead
        if j + 1 < len(tiles):
            ahead = first(tiles[j + 1])
        act, slope = gelu_parts(a)
        act = act.astype(bf16)
        h[:, cols] = act
        gp[:, cols] = slope
        term = dot_last(act, dn_s[:, cols])
        acc[...] = term if j == 0 else acc[...] + term


def ff_backward(dm, h, gp, up_s, dn_s, dbias, du, weights):
    tiles = [slice(j, j + TILE) for j in range(0, FF, TILE)]

    def first(cols):
        return dot(dm[...], dn_s[:, cols])

    ahead = first(tiles[0])
    for j, cols in enumerate(tiles):
        grad = ahead
        if j + 1 < len(tiles):
            ahead = first(tiles[j + 1])
        dpre = (grad * gp[:, cols]).astype(bf16)
        weights(cols, dpre)
        dbias[:, cols] = jnp.sum(dpre.astype(f32), 0, keepdims=True)
        term = dot_last(dpre, up_s[:, cols])
        du[...] = term if j == 0 else du[...] + term


def adam_update(weight, grad, first, second):
    first_new = adam_one * first + (1.0 - adam_one) * grad
    second_new = adam_two * second + (1.0 - adam_two) * grad * grad
    first_hat = first_new / (1.0 - adam_one**STEP)
    second_hat = second_new / (1.0 - adam_two**STEP)
    weight_new = weight * (1.0 - adam_rate * adam_decay) - adam_rate * first_hat / (
        jnp.sqrt(second_hat) + adam_floor
    )
    return (first_new, second_new, weight_new)


def flip(v):
    return v.astype(f32).T.astype(bf16)


def per_device(
    global_tokens,
    local_tokens,
    global_cotangent,
    local_cotangent,
    up_weight,
    down_weight,
    filters,
    resize,
    vectors,
    hidden_bias,
    up_momentum,
    down_momentum,
    filter_means,
    filter_squares,
    vector_means,
    vector_squares,
    bias_means,
    bias_squares,
):
    both = ("dp", "tensor")
    net = Net(lax.axis_size("dp"), lax.axis_size("tensor"))
    parts, across, devices = net.parts, net.across, net.devices
    micro, global_images = global_tokens.shape[:2]
    local_images = local_tokens.shape[1]
    layers, shard, cols = up_weight.shape
    direct = net.power and shard % 16 == 0 and cols == D
    plan = Plan(micro, global_images, local_images)
    rows, spec_rows = plan.rows, plan.spec
    to_tables = {k: jnp.asarray(t) for k, t in plan.tables.items()}
    filt = filters.reshape(layers, 2, GSPEC, D)
    down_t = jnp.swapaxes(down_weight, 1, 2)
    down_momentum_t = jnp.swapaxes(down_momentum, 1, 2)
    vec = jnp.swapaxes(vectors, 0, 1)
    vec_at = 2 * GSPEC
    bias_at = vec_at + 5
    adam_used = bias_at + FF // D
    share = round_up((adam_used + devices - 1) // devices, 8)
    adam_rows = devices * share if direct else round_up(adam_used, 8)
    matrix = struct((D, FF), bf16)
    row_f32 = struct((rows, D), f32)
    row_bf16 = struct((rows, D), bf16)
    column = struct((rows, 1), f32)
    flat = struct((D, rows), bf16)
    hidden = struct((rows, FF), bf16)
    hidden_f32 = struct((rows, FF), f32)
    unit = len(net.masks(1))
    inner = net.masks(2)
    inner1 = inner

    def piece_masks(inside):
        unit_at, size = net.stages[1]
        return [[c + i * unit_at + m for m in inside] for c in range(2) for i in range(size)]

    def whole(got):
        got = got.reshape(parts, across, -1, shard, cols)
        return got.transpose(2, 0, 3, 1, 4).reshape(got.shape[2], D, FF)

    def hold(current, token):
        return gate([current], token)[0] if direct else current

    def gather_near(current, later=None):
        if not direct:
            return far(whole(lax.all_gather(current.reshape(1, -1, cols), both, axis=0, tiled=True)))
        pieces = net.gather_plane(current)
        if later is not None:
            pieces = list(gate(pieces, later))
        return far(net.gather_core(pieces))

    def unpack(operand, inside, matrices, sem):
        if direct:
            pieces = list(zip(operand, piece_masks(inside)))
            place_blocks(net, net.me(), pieces, shard, cols, matrices, sem)
        else:
            for i, m in enumerate(matrices):
                start_copy(operand.at[i], m, sem.at[i])

    def arrived(matrices, sem):
        for i, m in enumerate(matrices):
            wait_copy(m, sem.at[i])

    def give(ins, matrices, outs, sem):
        if direct:
            cut_blocks(net, net.me(), shard, cols, matrices, outs, sem)
        else:
            for i, m in enumerate(matrices):
                start_copy(m, outs[i], sem.at[i])

    grad_shapes = [struct((unit, 2 * shard, D), bf16)] * 2 if direct else [matrix] * 2
    saved_shapes = Box(
        n1=row_f32, s1=column, spec=struct((spec_rows, D), f32), n2=row_f32, s2=column, u=row_bf16
    )
    norm_names = ("n1", "s1", "spec", "n2", "s2")
    chunk_shape = struct((1, 2 * shard, cols), bf16)

    def cast_body(ins, outs, s, sems):
        names = ("up", "dn")
        for i, name in enumerate(names):
            start_copy(ins[name], s[name], sems.given.at[i])
        for i, name in enumerate(names):
            wait_copy(s[name], sems.given.at[i])
            for layer, out in enumerate(outs.chunks):
                out[0, i * shard : (i + 1) * shard] = s[name][layer].astype(bf16)

    block_shape = struct((layers, shard, cols), f32)
    low_weights = call(
        cast_body,
        far(Box(up=up_weight, dn=down_t)),
        Box(chunks=[chunk_shape] * layers),
        Box(up=block_shape, dn=block_shape),
        Box(given=2),
        limit=8 * MIB,
    )
    reached = list(low_weights.chunks)
    if direct:
        reached[0] = net.gather_far(reached[0])
        reached[1], inner1 = net.gather_bits(gate([reached[1]], reached[0])[0])

    def pre_body(ins, outs, s, sems):
        for layer in range(layers):
            for c in range(2):
                outs.lk[layer, c] = dot(ins.resize[...], ins.filt[layer, c], high)
        for seg in plan.segments:
            load_rows(plan, seg, outs.x, ins.gt, ins.lt)
            load_rows(plan, seg, outs.dx, ins.gc, ins.lc)
        for kind, table in ins.to.items():
            outs.back_to[kind][...] = table[...].T
        tables = Box(to=ins.to, back_to=outs.back_to)
        pre_layer(plan, 0, outs.x, ins.vec, ins.filt, outs.lk, tables, **outs.saved)

    pre = call(
        pre_body,
        Box(
            gt=global_tokens, lt=local_tokens, gc=global_cotangent, lc=local_cotangent, vec=vec,
            filt=filt, resize=resize, to=to_tables,
        ),
        Box(
            x=row_f32, dx=row_f32, lk=struct((layers, 2, LSPEC, D), f32), saved=saved_shapes,
            back_to={k: struct(t.shape[::-1], f32) for k, t in to_tables.items()},
        ),
        limit=10 * MIB,
    )
    saved0, lk = pre.saved, pre.lk
    tables = Box(to=to_tables, back_to=pre.back_to)
    if direct:
        reached[1] = gate([reached[1]], lk)[0]
    weights0 = gather_near(reached[0], reached[1])
    reached1 = hold(reached[1], weights0[len(weights0) // 2 - 1].array) if direct else reached[1]

    def first_body(ins, outs, s, sems):
        unpack(ins.w, inner, outs.w, sems.w)
        arrived(outs.w, sems.w)
        ff_forward(0, ins.u, *outs.w, ins.bias, outs.h, outs.gp, s.acc)
        outs.x[...] = ins.x[...] + s.acc[...] + ins.vec[4, 0:1]

    first = call(
        first_body,
        Box(
            w=weights0, x=pre.x, u=saved0.u, vec=vec, bias=hidden_bias,
            token=far(reached1),
        ),
        Box(h=hidden, gp=hidden_f32, w=[matrix] * 2, x=row_f32),
        Box(acc=row_f32),
        Box(w=2),
        weight=9,
        limit=16 * MIB,
    )
    weights1 = gather_near(reached1, first.x)

    def middle_body(ins, outs, s, sems):
        pre_layer(plan, 1, ins.x, ins.vec, ins.filt, ins.lk, ins.tables, **outs)

    saved1 = call(
        middle_body,
        Box(x=first.x, vec=vec, filt=filt, lk=lk, tables=tables),
        saved_shapes,
        weight=4,
        limit=10 * MIB,
    )

    backward_scratch = Box(grads=[matrix] * 2, dmt=flat, ut=flat)

    def weight_gradients(s, grad, u, h):
        s.dmt[...] = grad.astype(f32).T.astype(bf16)
        s.ut[...] = flip(u[...])

        def tile(cols, dpre):
            s.grads[1][:, cols] = dot(s.dmt[...], h[:, cols]).astype(bf16)
            s.grads[0][:, cols] = dot(s.ut[...], dpre).astype(bf16)

        return tile

    def norms_back(layer, ins, du, dx, saved, tables_ref, shift, dbias, adam, out):
        sums, filt_sum = pre_layer_back(
            plan, layer, du, dx, ins.vec, ins.filt, ins.lk, tables_ref,
            dlk=ins.resize, **{k: saved[k] for k in norm_names},
        )
        for c in range(2):
            adam[c * GSPEC : (c + 1) * GSPEC] = filt_sum[c]
        for i in range(4):
            adam[vec_at + i : vec_at + i + 1] = sums[i]
        adam[vec_at + 4 : vec_at + 5] = shift[...]
        for i in range(FF // D):
            adam[bias_at + i : bias_at + i + 1] = dbias[:, i * D : (i + 1) * D]
        if adam_rows > adam_used:
            adam[adam_used:] = jnp.zeros((adam_rows - adam_used, D), f32)
        if direct:
            cut_adam(net, net.me(), share, adam, out)
        else:
            out[0][...] = adam[...]

    adam_shape = struct((adam_rows, D), f32)
    adam_shapes = [struct((unit, 2 * share, D), bf16)] * 2 if direct else [adam_shape]
    line = struct((1, D), f32)
    wide_line = struct((1, FF), f32)

    def second_body(ins, outs, s, sems):
        saved = ins.saved
        unpack(ins.w, inner1, s.w, sems.w)
        grad = ins.dx[...].astype(bf16)
        s.dm[...] = grad
        outs.shift[...] = jnp.sum(grad.astype(f32), 0, keepdims=True)
        tile = weight_gradients(s, grad, saved.u, s.h)
        arrived(s.w, sems.w)
        ff_forward(1, saved.u, *s.w, ins.bias, s.h, s.gp, s.acc)
        outs.y[...] = ins.x[...] + s.acc[...] + ins.vec[4, 1:2]
        ff_backward(s.dm, s.h, s.gp, *s.w, outs.dbias, outs.du, tile)
        give(ins, s.grads, outs.grads, sems.taken)
        arrived(s.grads, sems.taken)

    second = call(
        second_body,
        Box(w=weights1, x=first.x, saved=saved1, vec=vec, bias=hidden_bias, dx=pre.dx),
        Box(
            y=row_f32,
            grads=far(grad_shapes),
            du=row_f32,
            dbias=wide_line,
            shift=line,
        ),
        Box(acc=row_f32, h=hidden, gp=hidden_f32, w=[matrix] * 2, dm=row_bf16, **backward_scratch),
        Box(w=2, taken=2),
        weight=14,
        limit=25 * MIB,
    )

    def branch_body(ins, outs, s, sems):
        outs.dx[...] = ins.dx[...]
        norms_back(
            1, ins, ins.du, outs.dx, ins.saved, ins.tables, ins.shift, ins.dbias, s.adam, outs.adam
        )

    branch = call(
        branch_body,
        Box(
            du=second.du, dx=pre.dx, saved=saved1, shift=second.shift, dbias=second.dbias, vec=vec,
            filt=filt, lk=lk, resize=resize, tables=tables,
        ),
        Box(dx=row_f32, adam=adam_shapes),
        Box(adam=adam_shape),
        weight=3,
        limit=12 * MIB,
    )
    if direct:
        terms1 = net.exchange(0, second.grads)
        pairs1 = net.exchange(0, branch.adam)
        terms1 = sum_stage(terms1, pairs1, net.stages[1][1])
    else:
        terms1 = second.grads

    def third_body(ins, outs, s, sems):
        grad = ins.dx[...].astype(bf16)
        s.dm[...] = grad
        outs.shift[...] = jnp.sum(grad.astype(f32), 0, keepdims=True)
        tile = weight_gradients(s, grad, ins.u, ins.h)
        ff_backward(
            s.dm, ins.h, ins.gp, *ins.w, outs.dbias, outs.du, tile
        )
        give(ins, s.grads, outs.grads, sems.taken)
        arrived(s.grads, sems.taken)

    third = call(
        third_body,
        Box(
            w=first.w, dx=branch.dx, u=saved0.u, h=first.h, gp=first.gp, token=far(terms1[0])
        ),
        Box(grads=far(grad_shapes), du=row_f32, dbias=wide_line, shift=line),
        Box(dm=row_bf16, **backward_scratch),
        Box(taken=2),
        limit=12 * MIB,
    )
    grads0 = third.grads
    def fourth_body(ins, outs, s, sems):
        s.dx[...] = ins.dx[...]
        norms_back(
            0, ins, ins.du, s.dx, ins.saved, ins.tables, ins.shift,
            ins.dbias, s.adam, outs.adam,
        )
        for seg in plan.segments:
            store_rows(plan, seg, s.dx, outs.ggrad, outs.lgrad, False)
            store_rows(plan, seg, ins.y, outs.gout, outs.lout, True)

    fourth = call(
        fourth_body,
        Box(
            y=second.y,
            dx=branch.dx, du=third.du, dbias=third.dbias, shift=third.shift,
            saved={k: saved0[k] for k in norm_names}, vec=vec, filt=filt, lk=lk,
            resize=resize, tables=tables, token=far(terms1[0]),
        ),
        Box(
            gout=struct((global_images, TOKG, micro, D), bf16),
            lout=struct((micro, TOKL, local_images, D), bf16),
            ggrad=struct((micro, TOKG, global_images, D), f32),
            lgrad=struct((micro, TOKL, local_images, D), f32),
            adam=adam_shapes,
        ),
        Box(dx=row_f32, adam=adam_shape),
        limit=10 * MIB,
    )

    block = struct((shard, cols), f32)

    def momentum(layer, terms, token=(), others=None):
        if not direct:
            terms = jnp.stack(terms).reshape(2, parts, shard, across, cols)
            terms = terms.transpose(1, 3, 0, 2, 4).reshape(devices * 2, shard, cols)
            mine = lax.psum_scatter(terms, both, scatter_dimension=0, tiled=True).astype(f32)
            up = momentum_decay * up_momentum[layer] + mine[0]
            dn = momentum_decay * down_momentum_t[layer] + mine[1]
            return Box(up=up, dn=dn, chunk=jnp.concatenate([up, dn], 0).astype(bf16)[None])
        chunk = terms[0].shape[1]

        def body(ins, outs, s, sems):
            for i, name in enumerate(("up", "dn")):
                at = slice(i * shard, (i + 1) * shard)
                velocity = momentum_decay * ins[name][layer] + add_terms(ins.terms, (0, at))
                if others is None:
                    outs[name][...] = velocity
                else:
                    outs[name][layer] = velocity
                    outs[name][1 - layer] = ins.others[i][...]
                outs.chunk[0, at] = velocity.astype(bf16)
            outs.chunk[0, 2 * shard :] = pair(
                add_pairs(ins.terms, (0, slice(2 * shard, chunk)))
            )

        shape = block if others is None else block_shape
        return call(
            body,
            Box(
                terms=terms, up=up_momentum, dn=down_momentum_t, token=far(token),
                others=() if others is None else others,
            ),
            Box(up=shape, dn=shape, chunk=struct((1, chunk, D), bf16)),
            weight=0 if others is None else 20,
            limit=8 * MIB,
        )

    shown = [jnp.transpose(fourth.gout, (2, 0, 1, 3))] + [
        jnp.swapaxes(a, 1, 2) for a in (fourth.lout, fourth.ggrad, fourth.lgrad)
    ]
    if direct:
        cuts = [size for _, size in net.stages] + [1]
        terms1 = sum_stage(net.exchange(1, terms1), (), cuts[2], 2 * share, (), 20)
        terms0, pairs0 = net.exchange(0, grads0), net.exchange(0, fourth.adam)
        terms0 = sum_stage(terms0, pairs0, cuts[1], token=terms1[0])
        next0 = net.exchange(1, terms0)
        if len(net.stages) == 3:
            new1 = momentum(1, net.exchange(2, terms1), terms0[0])
            terms0 = sum_stage(next0, (), cuts[2], 2 * share, new1.chunk)
        else:
            terms0 = sum_stage(next0, (), cuts[2], 2 * share)
        for index in range(2, len(net.stages)):
            if index + 1 < len(net.stages):
                terms1 = net.exchange(index, terms1)
                terms1 = sum_stage(terms1, (), cuts[index + 1], 2 * share, terms0[0])
                terms0 = net.exchange(index, terms0)
                terms0 = sum_stage(terms0, (), cuts[index + 1], 2 * share, terms1[0])
        if len(net.stages) > 3:
            new1 = momentum(1, net.exchange(len(net.stages) - 1, terms1), terms0[0])
        new0 = momentum(
            0, net.exchange(len(net.stages) - 1, terms0), (), (new1.up, new1.dn)
        )
        reached1, inner1 = net.gather_bits(new1.chunk, (terms0[0], new0.chunk))
        up_velocity, down_velocity = new0.up, new0.dn
    else:
        new1 = momentum(1, terms1)
        new0 = momentum(0, grads0)
        up_velocity, down_velocity = (jnp.stack([new0[k], new1[k]]) for k in ("up", "dn"))

    scale_out = muon_rate * 0.2 * math.sqrt(max(D, FF))

    def eye():
        return (
            lax.broadcasted_iota(jnp.int32, (D, D), 0) == lax.broadcasted_iota(jnp.int32, (D, D), 1)
        ).astype(f32)

    def polynomial(gram, gram_s, poly_s, rows_at):
        one = eye()
        scale = 1.0 / (jnp.sqrt(jnp.sum(gram * one, keepdims=True)) + 1e-07)
        gram = gram * (scale * scale)
        gram_s[...] = gram
        poly_s[...] = ns_a * one + ns_b * gram + ns_c * dot(gram, gram, high)
        chain = [poly_s[rows_at]]
        for _ in range(2):
            row = chain[-1]
            for factor in (poly_s, gram_s, poly_s):
                row = dot(row, factor[...], high)
            chain.append(row)
        return (ns_a * chain[0] + ns_b * chain[1] + ns_c * chain[2]) * scale

    square = struct((D, D), f32)
    old = Box(up=up_weight, dn=down_t)
    names = ("up", "dn")

    def new_weight(old_weight, q_rows, v):
        orth = dot(q_rows, v)
        return old_weight * (1.0 - muon_rate * muon_decay) - scale_out * orth

    adam_ins = Box(
        filt=(filt, filter_means.reshape(filt.shape), filter_squares.reshape(filt.shape)),
        vec=(vec, jnp.swapaxes(vector_means, 0, 1), jnp.swapaxes(vector_squares, 0, 1)),
        bias=(hidden_bias, bias_means, bias_squares),
    )
    adam_shapes_out = jax.tree.map(lambda a: struct(a.shape, f32), adam_ins)
    adam_count = len(jax.tree.leaves(adam_ins))

    def adam_step(ins, outs, name, at, grad):
        old, mean, square = (ref[at] for ref in ins[name])
        for ref, value in zip(outs[name], adam_update(old, grad, mean, square)):
            ref[at] = value

    def adam_lines(ins, outs, layer, rows_at):
        for i in range(5):
            adam_step(ins, outs, "vec", (i, slice(layer, layer + 1)), rows_at(i))
        for i in range(FF // D):
            at = (slice(layer, layer + 1), slice(i * D, (i + 1) * D))
            adam_step(ins, outs, "bias", at, rows_at(5 + i))

    def copies(pairs, sems, action):
        for i, (src, dst) in enumerate(pairs):
            getattr(pltpu.make_async_copy(src, dst, sems.at[i]), action)()

    def muon_whole():
        moved = [
            whole(lax.all_gather(new.chunk[0].reshape(1, -1, cols), both, axis=0, tiled=True))
            for new in (new0, new1)
        ]
        start = lax.axis_index("dp") * shard

        def widen(weight):
            wide = jnp.zeros((layers, D, cols), f32)
            return lax.dynamic_update_slice_in_dim(wide, weight, start, 1)

        def body(ins, outs, s, sems):
            for layer in range(layers):
                total = ins.total.at[layer]
                for c in range(2):
                    rows_in = total[c * GSPEC : (c + 1) * GSPEC]
                    adam_step(ins.adam, outs.adam, "filt", (layer, c), rows_in)
                adam_lines(
                    ins.adam, outs.adam, layer, lambda i: total[vec_at + i : vec_at + i + 1]
                )
            cols_at = pl.ds(pl.multiple_of((net.me() % across) * cols, 128), cols)
            for layer in range(layers):
                for i, name in enumerate(names):
                    v = ins.v[layer][i]
                    q = polynomial(dot_last(v, v), s.gram, s.poly, slice(0, D))
                    part = ins.v[layer][i, :, cols_at]
                    outs[name][layer] = new_weight(ins.old[name][layer], q.astype(bf16), part)

        wide = struct((layers, D, cols), f32)
        last = call(
            body,
            Box(
                v=moved, old={k: widen(v) for k, v in old.items()}, adam=adam_ins,
                total=lax.psum(jnp.stack([fourth.adam[0], branch.adam[0]]), both),
            ),
            Box(up=wide, dn=wide, adam=adam_shapes_out),
            Box(gram=square, poly=square),
            limit=48 * MIB,
        )
        up, dn = (lax.dynamic_slice_in_dim(last[k], start, shard, 1) for k in names)
        return up, dn, last.adam

    def muon_direct():
        core_unit, far_unit = 1, 2
        half = D // 3
        places = [(0, 0), (0, 1), (0, 2), (1, 1), (1, 2), (2, 2)]
        tall = 2 * half
        far_bits = [2**b for b in range(2, net.bits) if 2**b < net.stages[1][0] * net.stages[1][1]]
        column_masks = []
        for masks in (inner, inner1):
            for bit in far_bits:
                masks = masks + [bit + m for m in masks]
            column_masks.append(masks)
        mine_rows = len(column_masks[0]) * share

        def pack(gram, out, start):
            for k, (r, c) in enumerate(places):
                at = pl.ds(start + (k // 3) * half, half)
                block_of = gram[r * half : (r + 1) * half, c * half : (c + 1) * half]
                out[at, (k % 3) * half : (k % 3 + 1) * half] = block_of.astype(bf16)

        def unpack_gram(terms, out):
            for k, (r, c) in enumerate(places):
                at = (pl.ds((k // 3) * half, half), pl.ds((k % 3) * half, half))
                value = terms[0][at].astype(f32) + terms[1][at].astype(f32)
                out[r * half : (r + 1) * half, c * half : (c + 1) * half] = value
                if r != c:
                    out[c * half : (c + 1) * half, r * half : (r + 1) * half] = value.T

        def gram_stage(layer, pieces, token):
            def body(ins, outs, s, sems):
                me_at = net.me()
                index = 0
                for array in ins.pieces:
                    for j in range(array.shape[0]):
                        d, _ = net.place(me_at, column_masks[layer][index])
                        at = pl.ds(pl.multiple_of(d * shard, 16), shard)
                        for i in range(2):
                            outs.v[i, at] = array[j, i * shard : (i + 1) * shard]
                        sums = add_pairs([array], (j, slice(2 * shard, 2 * shard + 2 * share)))
                        s.adam[index * share : (index + 1) * share] = sums
                        index += 1
                for i in range(2):
                    v = outs.v[i]
                    s.gram[i] = dot_last(v, v)
                core = me_at & 1
                pack(s.gram.at[core], outs.keep, 0)
                pack(s.gram.at[1 - core], outs.send, 0)
                rows_out = s.adam[...].astype(bf16)
                outs.send[tall:] = rows_out
                outs.adam[...] = rows_out

            return call(
                body,
                Box(pieces=pieces, token=far(token)),
                Box(
                    v=struct((2, D, cols), bf16),
                    keep=struct((tall, D), bf16),
                    adam=struct((mine_rows, D), bf16),
                    send=struct((tall + mine_rows, D), bf16),
                ),
                Box(gram=struct((2, D, D), f32), adam=struct((mine_rows, D), f32)),
                limit=16 * MIB,
            )

        def core_sum(keep, got, token):
            def body(ins, outs, s, sems):
                keep_ref, got_ref = ins.keep, ins.got
                outs[...] = (keep_ref[...].astype(f32) + got_ref[:tall].astype(f32)).astype(bf16)

            return call(
                body,
                Box(keep=keep, got=got, token=far(token)),
                struct((tall, D), bf16),
                limit=4 * MIB,
            )

        def pick_stage(keep, got, other):
            def body(ins, outs, s, sems):
                keep_ref, got_ref = ins.keep, ins.got
                x = (net.me() >> 1) & 1
                s.both[0] = (
                    keep_ref[...].astype(f32) + got_ref[:tall].astype(f32)
                ).astype(bf16)
                s.both[1] = ins.other[...]
                outs.mine[...] = s.both[x]
                outs.send[...] = s.both[1 - x]

            return call(
                body,
                Box(keep=keep, got=got, other=other),
                Box(mine=struct((tall, D), bf16), send=struct((tall, D), bf16)),
                Box(both=struct((2, tall, D), bf16)),
                limit=4 * MIB,
            )

        def poly_stage(mine, got):
            def body(ins, outs, s, sems):
                unpack_gram((ins.mine, ins.got), s.sum)
                d, _ = net.place(net.me(), 0)
                rows_at = pl.ds(pl.multiple_of(d * shard, 8), shard)
                q = polynomial(s.sum[...], s.gram, s.poly, rows_at)
                outs[...] = q.astype(bf16)

            return call(
                body,
                Box(mine=mine, got=got),
                struct((shard, D), bf16),
                Box(sum=square, gram=square, poly=square),
                weight=3,
                limit=8 * MIB,
            )

        def final_stage(vs, qs):
            def body(ins, outs, s, sems):
                at = net.me() & 3
                for mask, q in enumerate(ins.qs):
                    s.q[at ^ mask] = q[...]
                for layer in range(layers):
                    for i, name in enumerate(names):
                        q_rows = s.q[2 * layer + i]
                        outs[name][layer] = new_weight(
                            ins.old[name][layer], q_rows, ins.vs[layer][i]
                        )

            return call(
                body,
                Box(vs=vs, qs=qs, old=old),
                Box(up=block_shape, dn=block_shape),
                Box(q=struct((4, shard, D), bf16)),
                limit=6 * MIB,
            )

        line_rows = adam_rows - vec_at

        def mark_of(tree, key):
            marks = Box({k: jax.tree.map(lambda _: k == key, v) for k, v in tree.items()})
            return [i for i, mark in enumerate(jax.tree.leaves(marks)) if mark]

        def adam_stage(layer, columns, before, token=()):
            last = before is not None
            kinds = ("vec", "bias") if last else ()

            def body(ins, outs, s, sems):
                filts = [ref.at[layer] for ref in ins.adam.filt]
                filts_out = [ref.at[layer] for ref in outs.filt]
                whole_in = [(r, t) for k in kinds for r, t in zip(ins.adam[k], s.given[k])]
                loads = list(zip(filts, s.given.filt)) + whole_in
                copies(loads, sems.given, "start")
                for number, array in enumerate(ins.columns):
                    first_row = columns[number][1]
                    values = array[first_row : first_row + mine_rows].astype(f32)
                    for i, mask in enumerate(column_masks[layer]):
                        at = (net.me() ^ (mask | number)) * share
                        s.total[pl.ds(pl.multiple_of(at, 8), share)] = values[
                            i * share : (i + 1) * share
                        ]
                copies(loads, sems.given, "wait")
                for c in range(2):
                    grad = s.total[c * GSPEC : (c + 1) * GSPEC]
                    adam_step(s.given, s.taken, "filt", c, grad)
                stores = list(zip(s.taken.filt, filts_out))
                if last:
                    for number, ref, start in ((layer, s.total, vec_at), (1 - layer, ins.lines, 0)):
                        adam_lines(
                            s.given, s.taken, number,
                            lambda i, ref=ref, start=start: ref[start + i : start + i + 1],
                        )
                    stores += [(t, r) for k in kinds for t, r in zip(s.taken[k], outs[k])]
                else:
                    outs.lines[...] = s.total[vec_at:]
                copies(stores, sems.taken, "start")
                copies(stores, sems.taken, "wait")

            part = Box(filt=[struct(filt.shape[1:], f32)] * 3, **{k: adam_shapes_out[k] for k in kinds})
            ins = Box(adam=far(adam_ins), columns=[a for a, _ in columns], token=far(token))
            outs = Box(filt=far(list(adam_shapes_out.filt)))
            aliases = None
            if last:
                outs.update({k: far(adam_shapes_out[k]) for k in kinds})
                ins.lines = before.lines
                ins.done = far(before.filt)
                marks = mark_of(ins, "done")
                aliases = dict(zip(marks, mark_of(outs, "filt")))
            else:
                outs.lines = struct((line_rows, D), f32)
            count = 3 + 3 * len(kinds)
            return call(
                body,
                ins,
                outs,
                Box(given=part, taken=part, total=struct((adam_rows, D), f32)),
                Box(given=count, taken=count),
                weight=2,
                limit=8 * MIB,
                aliases=aliases,
            )

        def column(array):
            pieces = [array]
            for bit in far_bits:
                pieces = pieces + [net.swap(p, bit) for p in pieces]
            return pieces

        reached0 = net.gather_far(new0.chunk)
        gram1 = gram_stage(1, column(reached1), reached0)
        far1 = [net.swap(gram1.adam, mask) for mask in (2, 3)]
        gram0 = gram_stage(0, column(reached0), far1)
        got1, got0 = (net.swap(gram.send, core_unit) for gram in (gram1, gram0))
        rows1 = [(gram1.adam, 0), (got1, tall)] + [(a, 0) for a in far1]
        sum1 = core_sum(gram1.keep, got1, gram0.keep)
        picked = pick_stage(gram0.keep, got0, sum1)
        adam1 = adam_stage(1, rows1, None, picked.mine)
        q = poly_stage(picked.mine, net.swap(picked.send, far_unit))
        (late,) = gate([gram0.adam], adam1.lines)
        rows0 = [(late, 0), (got0, tall)] + [(net.swap(late, mask), 0) for mask in (2, 3)]
        adam_outs = adam_stage(0, rows0, adam1)
        qs = [q] + [net.swap(q, mask) for mask in (1, 2, 3)]
        final = final_stage([gram0.v, gram1.v], qs)
        return final.up, final.dn, adam_outs

    if direct:
        up_master, down_master, adam_outs = muon_direct()
    else:
        up_master, down_master, adam_outs = muon_whole()
    filter_mean, filter_square, filter_master = (
        a.reshape(filters.shape) for a in adam_outs.filt
    )
    vector_mean, vector_square, vector_master = (
        jnp.swapaxes(a, 0, 1) for a in adam_outs.vec
    )
    bias_mean, bias_square, bias_master = adam_outs.bias
    return (
        *shown,
        up_velocity,
        up_master,
        jnp.swapaxes(down_velocity, 1, 2),
        jnp.swapaxes(down_master, 1, 2),
        filter_mean,
        filter_square,
        filter_master,
        vector_mean,
        vector_square,
        vector_master,
        bias_mean,
        bias_square,
        bias_master,
    )


def solution(mesh):
    images = P(None, ("dp", "tensor"), None, None)
    up, down = P(None, "dp", "tensor"), P(None, "tensor", "dp")
    in_specs = (images,) * 4 + (up, down) + (P(),) * 4 + (up, down) + (P(),) * 6
    out_specs = (images,) * 4 + (up, up, down, down) + (P(),) * 9
    return jax.shard_map(
        per_device, mesh=mesh, in_specs=in_specs, out_specs=out_specs, check_vma=False
    )
```
